32 devices in a mesh: dp: 4 (over y, core), seq: 8 (over z, x).
Axes of the slice: x: 2, y: 2, z: 4, core: 2. Of those that a mesh axis runs over, the one named last changes fastest.
Arguments:
- tokens: bfloat16 [4, 1024, 2048], P('dp', 'seq'), may hold values from -6 to 6
- cotangent: bfloat16 [4, 1024, 2048], P('dp', 'seq'), may hold values from -6 to 6
- inner_weight: float32 [2048, 6144], P(('dp', 'seq')), may hold values from -0.125 to 0.125
- outer_weight: float32 [2048, 2048], P(('dp', 'seq')), may hold values from -0.75 to 0.75
- expand_weight: float32 [2048, 16384], P(('dp', 'seq')), may hold values from -0.125 to 0.125
- shrink_weight: float32 [8192, 2048], P(('dp', 'seq')), may hold values from -0.0625 to 0.0625
- norm_gains: float32 [2, 2048], P(None, ('dp', 'seq')), may hold values from 0.3 to 2.5
- first_inner: float32 [2048, 6144], P(('dp', 'seq')), may hold values from -0.00021362305 to 0.00021362305
- first_outer: float32 [2048, 2048], P(('dp', 'seq')), may hold values from -0.00021362305 to 0.00021362305
- first_expand: float32 [2048, 16384], P(('dp', 'seq')), may hold values from -0.00021362305 to 0.00021362305
- first_shrink: float32 [8192, 2048], P(('dp', 'seq')), may hold values from -0.00021362305 to 0.00021362305
- first_gains: float32 [2, 2048], P(None, ('dp', 'seq')), may hold values from -0.0017089844 to 0.0017089844
- second_inner: float32 [2048, 6144], P(('dp', 'seq')), may hold values from 8e-10 to 3.2e-09
- second_outer: float32 [2048, 2048], P(('dp', 'seq')), may hold values from 8e-10 to 3.2e-09
- second_expand: float32 [2048, 16384], P(('dp', 'seq')), may hold values from 8e-10 to 3.2e-09
- second_shrink: float32 [8192, 2048], P(('dp', 'seq')), may hold values from 8e-10 to 3.2e-09
- second_gains: float32 [2, 2048], P(None, ('dp', 'seq')), may hold values from 5e-08 to 2e-07
- document_index: int32 [4, 1024], P('dp', 'seq'), may hold values from 0 to 3, as said below
- group_order: int32 [16], replicated, may hold values from 0 to 15, as said below
Outputs:
- layer_output: float32 [4, 1024, 2048], P('dp', 'seq')
- input_gradient: float32 [4, 1024, 2048], P('dp', 'seq')
- global_norm: float32 [], replicated
- moment_inner: float32 [2048, 6144], P(('dp', 'seq'))
- moment_outer: float32 [2048, 2048], P(('dp', 'seq'))
- moment_expand: float32 [2048, 16384], P(('dp', 'seq'))
- moment_shrink: float32 [8192, 2048], P(('dp', 'seq'))
- moment_gains: float32 [2, 2048], P(None, ('dp', 'seq'))
- square_inner: float32 [2048, 6144], P(('dp', 'seq'))
- square_outer: float32 [2048, 2048], P(('dp', 'seq'))
- square_expand: float32 [2048, 16384], P(('dp', 'seq'))
- square_shrink: float32 [8192, 2048], P(('dp', 'seq'))
- square_gains: float32 [2, 2048], P(None, ('dp', 'seq'))
- master_inner: float32 [2048, 6144], P(('dp', 'seq'))
- master_outer: float32 [2048, 2048], P(('dp', 'seq'))
- master_expand: float32 [2048, 16384], P(('dp', 'seq'))
- master_shrink: float32 [8192, 2048], P(('dp', 'seq'))
- master_gains: float32 [2, 2048], P(None, ('dp', 'seq'))
The draws below stay inside these ranges and needn't reach their ends.
Inputs may be any that keep to these rules, and one draw needn't show every extreme that they name: `document_index`: In one sequence document 1 begins within the first 64 positions and ends within the last 64. `group_order`: each group number appears once.
All inputs are finite; a program needn't handle non-finite values.
Results may differ from the reference program's by a relative error of at most 0.015.
The reference program's roundings to bfloat16 on the way count: a program that leaves them out, or rounds other values in their place, can miss the bound.
Values may be sent and summed in bfloat16 or wider, within the bound.
No kernel may reach another device: no remote copies, remote signals or barrier semaphores. Data moves between devices by JAX's collectives and lax.ppermute only.
A program may use at most 576 MiB of HBM per device.

```python
import math
import jax
import jax.numpy as jnp
from jax import lax

D = 2048
HEADS = 16
FF = 8192
GROUP = 64
STEP = 10
HEAD = 128
LEN = 1024
SEQUENCES = 4
N_SEQ = 8


def shared_order(key):
    return jax.random.permutation(key, 2 * N_SEQ).astype(jnp.int32)


def draw_group_order(key, part):
    return shared_order(key)


def spread_cuts(single):
    return jnp.sort(jax.random.permutation(single, LEN - 1)[:3].astype(jnp.int32)) + 1


def draw_document_index(key, part):
    order = shared_order(key)
    key = jax.random.fold_in(key, 7)
    spread_keys = jax.random.split(jax.random.fold_in(key, 1), SEQUENCES)
    spread = jax.vmap(spread_cuts)(spread_keys).astype(jnp.int32)
    first_cut = jax.random.randint(jax.random.fold_in(key, 2), (), 1, GROUP, dtype=jnp.int32)
    second_cut = jax.random.randint(jax.random.fold_in(key, 3), (), LEN - GROUP + 1, LEN - 1, dtype=jnp.int32)
    third_cut = jax.random.randint(jax.random.fold_in(key, 4), (), second_cut + 1, LEN, dtype=jnp.int32)
    chosen = jax.random.randint(jax.random.fold_in(key, 5), (), 0, SEQUENCES, dtype=jnp.int32)
    long_cuts = jnp.stack([first_cut, second_cut, third_cut]).astype(jnp.int32)
    chosen_row = (jnp.arange(SEQUENCES, dtype=jnp.int32) == chosen)[:, None]
    cuts = jnp.where(chosen_row, long_cuts[None, :], spread)
    places = (order[:, None] * GROUP + jnp.arange(GROUP, dtype=jnp.int32)[None, :]).reshape(-1)
    ids = jnp.sum((places[None, :, None] >= cuts[:, None, :]).astype(jnp.int32), axis=2)
    return ids.astype(jnp.int32)


def draw_norm_gains(key, part):
    key = jax.random.fold_in(key, 5)
    ramp = jnp.arange(D, dtype=jnp.float32) / D
    base = 0.5 + ramp
    noise = jax.random.uniform(key, (2, D), jnp.float32, -0.1, 0.1)
    return base[None, :] * (1.0 + noise)


def levels(rng, shape, cuts, least, top_value):
    factor_of, own = 1.0, jax.random.fold_in(rng, 6)
    for dim, parts in cuts:
        draws = jnp.exp(jax.random.uniform(jax.random.fold_in(own, dim), (parts,), jnp.float32, least / len(cuts), top_value / len(cuts)))
        factor_of = factor_of * jnp.repeat(draws, shape[dim] // parts).reshape([-1 if axis == dim else 1 for axis in range(len(shape))])
    return factor_of


def centred(key, dims, deviation, reach, shards=(), held_as=jnp.bfloat16):
    entries = jax.random.normal(key, dims, jnp.float32) * deviation
    if len(shards) > 0:
        entries = levels(key, dims, shards, -0.22, 0.18) * entries
    return jnp.clip(entries, min=-reach, max=reach).astype(held_as)


def setup_inputs(seed: int = 0) -> dict:
    splits = jax.random.split(jax.random.key(seed), 20)
    return {
        "tokens": centred(splits[0], (SEQUENCES, LEN, D), 1.0, 6.0, ((0, 4), (1, 8))),
        "cotangent": centred(splits[1], (SEQUENCES, LEN, D), 1.0, 6.0, ((0, 4), (1, 8))),
        "inner_weight": centred(splits[2], (D, 3 * D), D ** -0.5, 0.125, ((0, 32),), jnp.float32),
        "outer_weight": centred(splits[3], (D, D), (D // 32) ** -0.5, 0.75, ((0, 32),), jnp.float32),
        "expand_weight": centred(splits[4], (D, 2 * FF), D ** -0.5, 0.125, ((0, 32),), jnp.float32),
        "shrink_weight": centred(splits[5], (FF, D), FF ** -0.5, 0.0625, ((0, 32),), jnp.float32),
        "norm_gains": draw_norm_gains(jax.random.fold_in(splits[19], 71), 0),
        "first_inner": centred(splits[7], (D, 3 * D), 0.0000136, 0.00021362305, ((0, 32),), jnp.float32),
        "first_outer": centred(splits[8], (D, D), 0.0000136, 0.00021362305, ((0, 32),), jnp.float32),
        "first_expand": centred(splits[9], (D, 2 * FF), 0.0000136, 0.00021362305, ((0, 32),), jnp.float32),
        "first_shrink": centred(splits[10], (FF, D), 0.0000136, 0.00021362305, ((0, 32),), jnp.float32),
        "first_gains": centred(splits[11], (2, D), 0.00011, 0.0017089844, ((1, 32),), jnp.float32),
        "second_inner": jnp.clip(jnp.exp(math.log(3.2000000427245823e-09) - 1.3862944 * jax.random.uniform(splits[12], (D, 3 * D), jnp.float32) ** levels(splits[12], (D, 3 * D), ((0, 32),), -0.2, 0.2)), 8.000000106811456e-10, 3.2000000427245823e-09),
        "second_outer": jnp.clip(jnp.exp(math.log(3.2000000427245823e-09) - 1.3862944 * jax.random.uniform(splits[13], (D, D), jnp.float32) ** levels(splits[13], (D, D), ((0, 32),), -0.2, 0.2)), 8.000000106811456e-10, 3.2000000427245823e-09),
        "second_expand": jnp.clip(jnp.exp(math.log(3.2000000427245823e-09) - 1.3862944 * jax.random.uniform(splits[14], (D, 2 * FF), jnp.float32) ** levels(splits[14], (D, 2 * FF), ((0, 32),), -0.2, 0.2)), 8.000000106811456e-10, 3.2000000427245823e-09),
        "second_shrink": jnp.clip(jnp.exp(math.log(3.2000000427245823e-09) - 1.3862944 * jax.random.uniform(splits[15], (FF, D), jnp.float32) ** levels(splits[15], (FF, D), ((0, 32),), -0.2, 0.2)), 8.000000106811456e-10, 3.2000000427245823e-09),
        "second_gains": jnp.clip(jnp.exp(math.log(2.0000000233721948e-07) - 1.3862944 * jax.random.uniform(splits[16], (2, D), jnp.float32) ** levels(splits[16], (2, D), ((1, 32),), -0.2, 0.2)), 5.000000058430487e-08, 2.0000000233721948e-07),
        "document_index": draw_document_index(jax.random.fold_in(splits[19], 71), 0),
        "group_order": draw_group_order(jax.random.fold_in(splits[19], 71), 0),
    }


EPSILON = 1e-05
THETA = 10000.0
BETA_ONE = 0.9
BETA_TWO = 0.95
RATE = 0.05
GAIN_RATE = 0.5
DECAY = 0.1
ADAM_EPSILON = 1e-08
CLIP = 1.0
HIGHEST = lax.Precision.HIGHEST

@jax.custom_vjp
def low(v):
    return lax.optimization_barrier(v.astype(jnp.bfloat16)).astype(jnp.float32)

@jax.custom_vjp
def low_back(v):
    return v

def low_keep(v):
    return (low(v), None)

def low_pass(kept, grad):
    return (grad,)

def back_keep(v):
    return (v, None)

def back_low(kept, grad):
    return (low(grad),)
low.defvjp(low_keep, low_pass)
low_back.defvjp(back_keep, back_low)

def matmul(left, right):
    return jnp.dot(left, right, precision=HIGHEST, preferred_element_type=jnp.float32)

def angles(positions, width):
    frequency = THETA ** (-(jnp.arange(width // 2, dtype=jnp.float32) * 2.0) / width)
    turned = positions.astype(jnp.float32)[:, None] * frequency[None, :]
    return (jnp.cos(turned)[:, None, :], jnp.sin(turned)[:, None, :])

def rotate(values, cosine, sine):
    half = values.shape[-1] // 2
    first, second = (values[..., :half], values[..., half:])
    return jnp.concatenate([first * cosine - second * sine, second * cosine + first * sine], axis=-1)

def attend(queries, keys, values, documents, positions):
    block = math.gcd(LEN, 512)

    def one_block(start):
        rows_query = lax.dynamic_slice_in_dim(queries, start, block, 0)
        place_query = lax.dynamic_slice_in_dim(positions, start, block, 0)
        document_query = lax.dynamic_slice_in_dim(documents, start, block, 0)
        scores = jnp.einsum('qhd,khd->hqk', rows_query, keys, precision=HIGHEST) * HEAD ** (-0.5) - math.log(LEN)
        scores = low_back(scores)
        visible = ((document_query[:, None] == documents[None, :]) & (positions[None, :] <= place_query[:, None])).astype(jnp.float32)
        weights = low(jax.nn.sigmoid(scores) * visible[None])
        return jnp.einsum('hqk,khd->qhd', weights, values, precision=HIGHEST)
    starts = jnp.arange(0, LEN, block).astype(jnp.int32)
    blocks = lax.map(jax.checkpoint(one_block), starts)
    return blocks.reshape(LEN, HEADS, HEAD)

def layer(inputs, params, documents, positions):
    inner = low(params[0])
    outer = low(params[1])
    expand = low(params[2])
    shrink = low(params[3])
    gains = low(params[4])
    cosine, sine = angles(positions, HEAD)

    def one_sequence(carry, pieces):
        rows_in, document_row = pieces
        inverse_first = lax.rsqrt(lax.optimization_barrier(jnp.mean(rows_in * rows_in, axis=-1, keepdims=True)) + EPSILON)
        attend_input = low(rows_in * inverse_first * gains[0])
        projected = low_back(matmul(attend_input, inner))
        queries = projected[:, :D].reshape(LEN, HEADS, HEAD)
        keys = projected[:, D:2 * D].reshape(LEN, HEADS, HEAD)
        values = projected[:, 2 * D:].reshape(LEN, HEADS, HEAD)
        query_rot = low(rotate(queries, cosine, sine))
        key_rot = low(rotate(keys, cosine, sine))
        value_low = low(values)
        attended = attend(query_rot, key_rot, value_low, document_row, positions)
        attended = low_back(low(attended.reshape(LEN, D)))
        residual = rows_in + low_back(matmul(attended, outer))
        inverse_second = lax.rsqrt(lax.optimization_barrier(jnp.mean(residual * residual, axis=-1, keepdims=True)) + EPSILON)
        mlp_input = low(residual * inverse_second * gains[1])
        gate_up = low_back(matmul(mlp_input, expand))
        gate, upward = (gate_up[:, :FF], gate_up[:, FF:])
        activation = low(jax.nn.silu(gate) * upward)
        output = residual + low_back(matmul(activation, shrink))
        return (carry, output)
    carry, outputs = lax.scan(one_sequence, None, (inputs, documents))
    return outputs

def adamw(weight, grad, first, second, factor, decay, rate):
    grad = grad * factor
    first = BETA_ONE * first + (1.0 - BETA_ONE) * grad
    second = BETA_TWO * second + (1.0 - BETA_TWO) * grad * grad
    update = first / (1.0 - BETA_ONE ** STEP) / (jnp.sqrt(second / (1.0 - BETA_TWO ** STEP)) + ADAM_EPSILON)
    return (first, second, weight - rate * (update + decay * weight))

def reference(tokens, cotangent, inner_weight, outer_weight, expand_weight, shrink_weight, norm_gains, first_inner, first_outer, first_expand, first_shrink, first_gains, second_inner, second_outer, second_expand, second_shrink, second_gains, document_index, group_order):
    positions = (group_order[:, None] * GROUP + jnp.arange(GROUP).astype(jnp.int32)[None, :]).reshape(-1).astype(jnp.int32)
    params = (inner_weight, outer_weight, expand_weight, shrink_weight, norm_gains)

    def run(inputs, weights):
        return layer(inputs, weights, document_index, positions)
    layer_output, pull = jax.vjp(run, tokens.astype(jnp.float32), params)
    input_gradient, grads = pull(cotangent.astype(jnp.float32))
    total = jnp.sum(grads[0] * grads[0]) + jnp.sum(grads[1] * grads[1]) + jnp.sum(grads[2] * grads[2])
    total = total + jnp.sum(grads[3] * grads[3]) + jnp.sum(grads[4] * grads[4])
    global_norm = jnp.sqrt(total)
    factor = CLIP / jnp.maximum(global_norm, CLIP)
    firsts = (first_inner, first_outer, first_expand, first_shrink, first_gains)
    seconds = (second_inner, second_outer, second_expand, second_shrink, second_gains)
    decays = (DECAY, DECAY, DECAY, DECAY, 0.0)
    rates = (RATE, RATE, RATE, RATE, GAIN_RATE)
    results = [adamw(params[i], grads[i], firsts[i], seconds[i], factor, decays[i], rates[i]) for i in range(5)]
    return (layer_output, input_gradient, global_norm, results[0][0], results[1][0], results[2][0], results[3][0], results[4][0], results[0][1], results[1][1], results[2][1], results[3][1], results[4][1], results[0][2], results[1][2], results[2][2], results[3][2], results[4][2])
```

```python
import math

import jax
import jax.numpy as jnp
from jax import lax
from jax.sharding import PartitionSpec as P

HEADS = 16
STEP = 10


EPSILON = 1e-05
THETA = 10000.0
BETA_ONE = 0.9
BETA_TWO = 0.95
RATE = 0.05
GAIN_RATE = 0.5
DECAY = 0.1
ADAM_EPSILON = 1e-08
CLIP = 1.0
BOTH = ("dp", "seq")


def angles(positions, width):
    frequency = THETA ** (-(jnp.arange(width // 2, dtype=jnp.float32) * 2.0) / width)
    turned = positions.astype(jnp.float32)[:, None] * frequency[None, :]
    return (jnp.cos(turned)[:, None, :], jnp.sin(turned)[:, None, :])


def rotate(values, cosine, sine):
    half = values.shape[-1] // 2
    first, second = (values[..., :half], values[..., half:])
    return jnp.concatenate(
        [first * cosine - second * sine, second * cosine + first * sine], axis=-1
    )


def unrotate(upstream, cosine, sine):
    half = upstream.shape[-1] // 2
    first, second = (upstream[..., :half], upstream[..., half:])
    return jnp.concatenate(
        [first * cosine + second * sine, second * cosine - first * sine], axis=-1
    )


def norm_back(upstream, normed, inverse):
    return inverse * (upstream - normed * jnp.mean(upstream * normed, axis=-1, keepdims=True))


def contract_rows(left, right):
    return lax.dot_general(
        left, right, (((0,), (0,)), ((), ())), preferred_element_type=jnp.float32
    )


def contract_last(left, right):
    return lax.dot_general(
        left, right, (((1,), (1,)), ((), ())), preferred_element_type=jnp.float32
    )


def multiply(left, right):
    return jnp.dot(left, right, preferred_element_type=jnp.float32)


def adamw(weight, grad, first, second, factor, decay, rate):
    grad = grad * factor
    first = BETA_ONE * first + (1.0 - BETA_ONE) * grad
    second = BETA_TWO * second + (1.0 - BETA_TWO) * grad * grad
    update = (
        first / (1.0 - BETA_ONE**STEP) / (jnp.sqrt(second / (1.0 - BETA_TWO**STEP)) + ADAM_EPSILON)
    )
    return (first, second, weight - rate * (update + decay * weight))


def move(value, where):
    pairs = []
    for dp in range(lax.axis_size("dp")):
        for seq in range(lax.axis_size("seq")):
            target = where(dp, seq // 2, seq % 2)
            if target is not None:
                pairs.append(
                    (
                        dp * lax.axis_size("seq") + seq,
                        target[0] * lax.axis_size("seq") + target[1] * 2 + target[2],
                    )
                )
    return lax.ppermute(value, BOTH, pairs)


def depth_of():
    return lax.axis_size("seq") // 2


def across(value):
    return move(value, lambda dp, z, x: (dp, z, 1 - x))


def turn(value, k):
    depth = depth_of()
    return move(value, lambda dp, z, x: (dp, (z + k) % depth, x))


def line(value, hop, direction):
    depth = depth_of()

    def where(dp, z, x):
        if direction > 0:
            return (dp, z + 1, x) if z >= hop - 1 and z + 1 < depth else None
        return (dp, z - 1, x) if z <= depth - hop and z >= 1 else None

    return move(value, where)


def across_from(value, hop, direction):
    depth = depth_of()

    def where(dp, z, x):
        valid = z >= hop if direction > 0 else z + hop < depth
        return (dp, z, 1 - x) if valid else None

    return move(value, where)


def gather_rows(block):
    depth = depth_of()
    z = lax.axis_index("seq") // 2
    up, down = [block], [block]
    for hop in range(1, depth):
        up.append(line(up[-1], hop, 1))
        down.append(line(down[-1], hop, -1))
    pieces = [jnp.concatenate([block, across(block)], axis=0)]
    up_across = [None] + [across_from(up[k], k, 1) for k in range(1, depth)]
    down_across = [None] + [across_from(down[k], k, -1) for k in range(1, depth)]
    for k in range(1, depth):
        pieces.append(
            jnp.where(
                z >= k,
                jnp.concatenate([up[k], up_across[k]], axis=0),
                jnp.concatenate([down[depth - k], down_across[depth - k]], axis=0),
            )
        )
    return pieces


def gather_small(block):
    depth = depth_of()
    column = jnp.stack([block] + [turn(block, k) for k in range(1, depth)])
    other = across(column)
    return jnp.stack([column, other], axis=1)


def scatter_rows(partial):
    depth = depth_of()
    order = sorted(range(1, depth), key=lambda k: -min(k, depth - k)) + [0]
    sums = {}
    for k in order:
        term = partial(k)
        rows = term.shape[0] // 2
        received = across(term[rows:])
        total = term[:rows].astype(jnp.float32) + received.astype(jnp.float32)
        sums[k] = turn(total.astype(jnp.bfloat16), -k).astype(jnp.float32) if k else total
    total = sums[0]
    for k in range(1, depth):
        total = total + sums[k]
    return total


def sum_everywhere(value):
    for stride in range(2):
        value = value + move(value, lambda dp, z, x: (dp ^ (1 << stride), z, x))
    for stride in range((depth_of() - 1).bit_length()):
        value = value + move(value, lambda dp, z, x: (dp, z ^ (1 << stride), x))
    return value + across(value)


def swap(value):
    return move(value, lambda dp, z, x: (x * 2 + dp % 2, z, dp // 2))


def exchange(chunks):
    return lax.all_to_all(chunks, "seq", 0, 0, tiled=True)


def share(rows):
    return lax.all_gather(rows, "dp", axis=0, tiled=True)


def reduce_over(rows):
    return lax.psum_scatter(rows, "dp", scatter_dimension=0, tiled=True)


def body(
    tokens,
    cotangent,
    inner_weight,
    outer_weight,
    expand_weight,
    shrink_weight,
    norm_gains,
    first_inner,
    first_outer,
    first_expand,
    first_shrink,
    first_gains,
    second_inner,
    second_outer,
    second_expand,
    second_shrink,
    second_gains,
    document_index,
    group_order,
):
    bf16, f32 = jnp.bfloat16, jnp.float32
    rows, width = tokens.shape[1:]
    n_dp, n_seq = lax.axis_size("dp"), lax.axis_size("seq")
    depth = depth_of()
    head = width // HEADS
    own_heads = HEADS // n_seq
    owned = inner_weight.shape[0]
    length = rows * n_seq
    scale = head ** (-0.5)
    offset = -math.log(length)
    group = rows // 2
    hidden = expand_weight.shape[1] // 2
    slab = shrink_weight.shape[0]
    device = lax.axis_index(BOTH)
    z, x = lax.axis_index("seq") // 2, lax.axis_index("seq") % 2

    inputs_low = tokens[0]
    upstream = cotangent[0]

    inner_chunks = inner_weight.astype(bf16).reshape(owned, 3, 2, own_heads, depth, head)
    inner_chunks = inner_chunks.transpose(4, 2, 0, 1, 3, 5).reshape(
        n_seq, owned, 3 * own_heads * head
    )
    inner = share(exchange(inner_chunks).reshape(n_seq * owned, -1))
    outer = share(swap(outer_weight.astype(bf16)))
    outer = outer.reshape(2, own_heads, owned, width).transpose(1, 0, 2, 3).reshape(-1, width)
    expand_chunks = expand_weight.astype(bf16).reshape(owned, 2, n_dp, n_seq, slab)
    expand_chunks = expand_chunks.transpose(3, 0, 1, 2, 4).reshape(n_seq, owned, 2 * n_dp * slab)
    expand = share(exchange(expand_chunks).reshape(n_seq * owned, -1))
    shrink = share(shrink_weight.astype(bf16))

    gains = lax.dynamic_update_slice(
        jnp.zeros((2, width), f32),
        norm_gains.astype(bf16).astype(f32),
        (jnp.int32(0), device * norm_gains.shape[1]),
    )
    gains = sum_everywhere(gains)
    gain_one, gain_two = gains[0], gains[1]

    sources = [((z - k) % depth) * 2 + (x ^ j) for k in range(depth) for j in range(2)]
    groups = jnp.concatenate([lax.dynamic_slice_in_dim(group_order, 2 * s, 2) for s in sources])
    within = jnp.arange(group, dtype=jnp.int32)
    places = (groups[:, None] * group + within[None, :]).reshape(-1)
    documents = gather_small(document_index[0]).reshape(-1)
    cosine, sine = angles(places, head)

    def first_norm(piece):
        values = piece.astype(f32)
        inverse = lax.rsqrt(jnp.mean(values * values, axis=-1, keepdims=True) + EPSILON)
        return values * inverse, inverse

    token_pieces = gather_rows(inputs_low)
    attend_pieces = [(first_norm(piece)[0] * gain_one).astype(bf16) for piece in token_pieces]
    projected = jnp.concatenate([multiply(piece, inner) for piece in attend_pieces], axis=0)
    projected = projected.reshape(length, 3, own_heads, head)
    query_rot = rotate(projected[:, 0], cosine, sine).astype(bf16)
    key_rot = rotate(projected[:, 1], cosine, sine).astype(bf16)
    value_low = projected[:, 2].astype(bf16)

    visible = (documents[:, None] == documents[None, :]) & (places[None, :] <= places[:, None])
    visible = visible.astype(f32)[None]

    def heads_dot(spec, left, right):
        return jnp.einsum(spec, left, right, preferred_element_type=f32)

    scores = heads_dot("qhd,khd->hqk", query_rot, key_rot) * scale + offset
    weights = jax.nn.sigmoid(scores) * visible
    weights_low = weights.astype(bf16)
    attended = heads_dot("hqk,khd->qhd", weights_low, value_low)
    attended = attended.reshape(length, own_heads * head).astype(bf16)

    def rows_of(array, k):
        return array[2 * rows * k : 2 * rows * (k + 1)]

    branch = scatter_rows(lambda k: multiply(rows_of(attended, k), outer).astype(bf16))
    inputs = inputs_low.astype(f32)
    residual = inputs + branch
    inverse_second = lax.rsqrt(jnp.mean(residual * residual, axis=-1, keepdims=True) + EPSILON)
    normed_second = residual * inverse_second

    upstream_pieces = gather_rows(upstream)
    mlp_pieces = gather_rows((normed_second * gain_two).astype(bf16))
    share_hidden = hidden // n_seq

    activations, gate_up_grads = [None] * depth, [None] * depth

    def feed_back(k):
        gate_up = multiply(mlp_pieces[k], expand)
        gate, upward = gate_up[:, :share_hidden], gate_up[:, share_hidden:]
        squash = jax.nn.sigmoid(gate)
        activations[k] = (gate * squash * upward).astype(bf16)
        down_grad = contract_last(upstream_pieces[k], shrink)
        d_gate = down_grad * upward * squash * (1.0 + gate * (1.0 - squash))
        d_upward = down_grad * gate * squash
        gate_up_grads[k] = jnp.concatenate([d_gate, d_upward], axis=1).astype(bf16)
        return contract_last(gate_up_grads[k], expand).astype(bf16)

    d_mlp_input = scatter_rows(feed_back)
    feed = scatter_rows(lambda k: multiply(activations[k], shrink).astype(bf16))
    output = residual + feed
    upstream_all = jnp.concatenate(upstream_pieces, axis=0)
    grad_shrink = reduce_over(
        contract_rows(jnp.concatenate(activations, axis=0), upstream_all).astype(bf16)
    )
    grad_expand = contract_rows(
        jnp.concatenate(mlp_pieces, axis=0), jnp.concatenate(gate_up_grads, axis=0)
    )
    grad_expand = reduce_over(grad_expand.astype(bf16))

    partial_gain_two = jnp.sum(d_mlp_input * normed_second, axis=0)
    d_residual = upstream.astype(f32) + norm_back(
        d_mlp_input * gain_two, normed_second, inverse_second
    )

    residual_pieces = gather_rows(d_residual.astype(bf16))
    d_attended = jnp.concatenate(
        [contract_last(piece, outer) for piece in residual_pieces], axis=0
    ).astype(bf16)
    grad_outer = contract_rows(attended, jnp.concatenate(residual_pieces, axis=0)).astype(bf16)
    grad_outer = grad_outer.reshape(own_heads, 2, owned, width).transpose(1, 0, 2, 3)
    grad_outer = reduce_over(grad_outer.reshape(-1, width))
    d_attended = d_attended.reshape(length, own_heads, head)
    d_weights = heads_dot("qhd,khd->hqk", d_attended, value_low)
    d_scores = (d_weights * weights * (1.0 - weights)).astype(bf16)
    d_query = heads_dot("hqk,khd->qhd", d_scores, key_rot) * scale
    d_key = heads_dot("hqk,qhd->khd", d_scores, query_rot) * scale
    d_value = heads_dot("hqk,qhd->khd", weights_low, d_attended)
    d_projected = jnp.stack(
        [unrotate(d_query, cosine, sine), unrotate(d_key, cosine, sine), d_value], axis=1
    )
    d_projected = d_projected.reshape(length, -1).astype(bf16)
    d_attend_input = scatter_rows(
        lambda k: contract_last(rows_of(d_projected, k), inner).astype(bf16)
    )
    grad_inner = contract_rows(jnp.concatenate(attend_pieces, axis=0), d_projected)
    grad_inner = reduce_over(grad_inner.astype(bf16))

    normed_first, inverse_first = first_norm(inputs_low)
    partial_gain_one = jnp.sum(d_attend_input * normed_first, axis=0)
    input_gradient = d_residual + norm_back(d_attend_input * gain_one, normed_first, inverse_first)

    local_squares = sum(
        jnp.sum(jnp.square(grad.astype(f32)))
        for grad in (grad_inner, grad_outer, grad_expand, grad_shrink)
    )
    sums = sum_everywhere(
        jnp.concatenate(
            [partial_gain_one, partial_gain_two, jnp.full((128,), local_squares)]
        ).reshape(-1, 128)
    ).reshape(-1)
    gains_whole = sums[: 2 * width].reshape(2, width)
    grad_gains = lax.dynamic_slice_in_dim(
        gains_whole, device * norm_gains.shape[1], norm_gains.shape[1], 1
    )
    global_norm = jnp.sqrt(sums[2 * width] + jnp.sum(gains_whole * gains_whole))
    factor = CLIP / jnp.maximum(global_norm, CLIP)

    grad_inner = exchange(grad_inner.reshape(n_seq, owned, -1))
    grad_inner = grad_inner.reshape(depth, 2, owned, 3, own_heads, head)
    grad_inner = grad_inner.transpose(2, 3, 1, 4, 0, 5).reshape(inner_weight.shape)
    grad_outer = swap(grad_outer)
    grad_expand = exchange(grad_expand.reshape(n_seq, owned, -1))
    grad_expand = grad_expand.reshape(n_seq, owned, 2, n_dp, slab)
    grad_expand = grad_expand.transpose(1, 2, 3, 0, 4).reshape(expand_weight.shape)

    gradients = (grad_inner, grad_outer, grad_expand, grad_shrink, grad_gains)
    masters = (inner_weight, outer_weight, expand_weight, shrink_weight, norm_gains)
    firsts = (first_inner, first_outer, first_expand, first_shrink, first_gains)
    seconds = (second_inner, second_outer, second_expand, second_shrink, second_gains)
    decays = (DECAY, DECAY, DECAY, DECAY, 0.0)
    rates = (RATE, RATE, RATE, RATE, GAIN_RATE)
    results = [
        adamw(
            masters[index],
            gradients[index].astype(f32),
            firsts[index],
            seconds[index],
            factor,
            decays[index],
            rates[index],
        )
        for index in range(5)
    ]
    return (
        output[None],
        input_gradient[None],
        global_norm,
        *(result[0] for result in results),
        *(result[1] for result in results),
        *(result[2] for result in results),
    )


def project_in(normed, weight, gain):
    rows = normed.shape[0]

    def add_piece(carry, pieces, start):
        piece_left = (normed * pieces[1].astype(jnp.float32)).astype(jnp.bfloat16)
        partial_sum = jnp.dot(piece_left, pieces[0], preferred_element_type=jnp.float32)
        return (partial_sum, pieces[1])

    initial = (
        jnp.zeros((rows, weight.shape[1]), jnp.float32),
        jnp.zeros((normed.shape[1],), jnp.bfloat16),
    )
    product, full_gain = add_piece(
        initial,
        (
            lax.all_gather(weight.astype(jnp.bfloat16), ("dp", "seq"), axis=0, tiled=True),
            lax.all_gather(gain.astype(jnp.bfloat16), ("dp", "seq"), axis=0, tiled=True),
        ),
        jnp.int32(0),
    )
    left = (normed * full_gain.astype(jnp.float32)).astype(jnp.bfloat16)
    return (product, left, None, full_gain.astype(jnp.float32))


def project_mid(left, weight):

    def add_piece(partial_sum, piece, start):
        return jnp.dot(left, piece, preferred_element_type=jnp.float32)

    initial = jnp.zeros((left.shape[0], weight.shape[1]), jnp.float32)
    product = add_piece(
        initial,
        lax.all_gather(weight.astype(jnp.bfloat16), ("dp", "seq"), axis=0, tiled=True),
        jnp.int32(0),
    )
    return (product, None)


def weights_back(upstream, weight):
    return contract_last(
        upstream, lax.all_gather(weight.astype(jnp.bfloat16), ("dp", "seq"), axis=0, tiled=True)
    )


def reduce_in(left, upstream):
    owned = left.shape[1] // lax.axis_size(("dp", "seq"))

    def term(start, count):
        return contract_rows(left, upstream)

    return lax.psum_scatter(
        term(jnp.int32(0), lax.axis_size(("dp", "seq")) * owned),
        ("dp", "seq"),
        scatter_dimension=0,
        tiled=True,
    )


def reduce_mid(left, upstream):
    owned = left.shape[1] // lax.axis_size(("dp", "seq"))

    def term(start, count):
        return contract_rows(left, upstream)

    return lax.psum_scatter(
        term(jnp.int32(0), lax.axis_size(("dp", "seq")) * owned),
        ("dp", "seq"),
        scatter_dimension=0,
        tiled=True,
    )


def gathered_body(
    tokens,
    cotangent,
    inner_weight,
    outer_weight,
    expand_weight,
    shrink_weight,
    norm_gains,
    first_inner,
    first_outer,
    first_expand,
    first_shrink,
    first_gains,
    second_inner,
    second_outer,
    second_expand,
    second_shrink,
    second_gains,
    document_index,
    group_order,
):
    inputs = tokens[0].astype(jnp.float32)
    rows, width = inputs.shape
    head_size = width // HEADS
    length = rows * lax.axis_size("seq")
    scale = head_size ** (-0.5)
    offset = -math.log(length)
    group = rows // 2
    within = jnp.arange(group, dtype=jnp.int32)
    paired = lax.dynamic_slice_in_dim(group_order, 2 * lax.axis_index("seq"), 2)
    own_place = (paired[:, None] * group + within[None, :]).reshape(-1)
    all_places = (group_order[:, None] * group + within[None, :]).reshape(-1)
    own_document = document_index[0].astype(jnp.bfloat16)
    cosine, sine = angles(own_place, head_size)
    inverse_first = lax.rsqrt(jnp.mean(inputs * inputs, axis=-1, keepdims=True) + EPSILON)
    normed_first = inputs * inverse_first
    projected, attend_input, kept_inner, gain_one = project_in(
        normed_first, inner_weight, norm_gains[0]
    )
    queries = projected[:, :width].reshape(rows, HEADS, head_size)
    query_rot = rotate(queries, cosine, sine).astype(jnp.bfloat16)
    key_rot = rotate(projected[:, width : 2 * width].reshape(rows, HEADS, head_size), cosine, sine)
    key_rot = key_rot.reshape(rows, width).astype(jnp.bfloat16)
    value_low = projected[:, 2 * width :].astype(jnp.bfloat16)

    def sigmoid_weights(key_piece, document_piece):
        count = key_piece.shape[0]
        scores = (
            jnp.einsum(
                "qhd,khd->hqk",
                query_rot,
                key_piece.reshape(count, HEADS, head_size),
                preferred_element_type=jnp.float32,
            )
            * scale
            + offset
        )
        visible = (own_document[:, None] == document_piece[None, :]) & (
            all_places[None, :] <= own_place[:, None]
        )
        return jax.nn.sigmoid(scores) * visible.astype(jnp.float32)[None]

    key_piece = lax.all_gather(key_rot, "seq", axis=0, tiled=True)
    value_piece = lax.all_gather(value_low, "seq", axis=0, tiled=True)
    document_piece = lax.all_gather(own_document, "seq", axis=0, tiled=True)
    count = key_piece.shape[0]
    weights = sigmoid_weights(key_piece, document_piece).astype(jnp.bfloat16)
    attended = jnp.einsum(
        "hqk,khd->qhd",
        weights,
        value_piece.reshape(count, HEADS, head_size),
        preferred_element_type=jnp.float32,
    )
    attended = attended.reshape(rows, width).astype(jnp.bfloat16)
    branch, kept_outer = project_mid(attended, outer_weight)
    residual = inputs + branch
    inverse_second = lax.rsqrt(jnp.mean(residual * residual, axis=-1, keepdims=True) + EPSILON)
    normed_second = residual * inverse_second
    gate_up, mlp_input, kept_expand, gain_two = project_in(
        normed_second, expand_weight, norm_gains[1]
    )
    hidden = gate_up.shape[1] // 2
    gate = gate_up[:, :hidden]
    upward = gate_up[:, hidden:]
    squash = jax.nn.sigmoid(gate)
    activation = (gate * squash * upward).astype(jnp.bfloat16)
    feed, kept_shrink = project_mid(activation, shrink_weight)
    output = residual + feed
    upstream = cotangent[0]
    down_grad = weights_back(upstream, shrink_weight)
    grad_shrink = reduce_mid(activation, upstream)
    d_gate = down_grad * upward * squash * (1.0 + gate * (1.0 - squash))
    d_upward = down_grad * gate * squash
    d_gate_up = jnp.concatenate([d_gate, d_upward], axis=1).astype(jnp.bfloat16)
    d_mlp_input = weights_back(d_gate_up, expand_weight)
    grad_expand = reduce_in(mlp_input, d_gate_up)
    partial_gain_two = jnp.sum(d_mlp_input * normed_second, axis=0)
    d_residual = upstream.astype(jnp.float32) + norm_back(
        d_mlp_input * gain_two, normed_second, inverse_second
    )
    d_residual_low = d_residual.astype(jnp.bfloat16)
    d_attended = weights_back(d_residual_low, outer_weight)
    grad_outer = reduce_mid(attended, d_residual_low)
    d_attended_flat = d_attended.astype(jnp.bfloat16)
    d_attended_low = d_attended_flat.reshape(rows, HEADS, head_size)
    key_piece = lax.all_gather(key_rot, "seq", axis=0, tiled=True)
    value_piece = lax.all_gather(value_low, "seq", axis=0, tiled=True)
    document_piece = lax.all_gather(own_document, "seq", axis=0, tiled=True)
    count = key_piece.shape[0]
    score_count = key_piece.shape[0]
    weights = sigmoid_weights(key_piece, document_piece)
    d_weights = jnp.einsum(
        "qhd,khd->hqk",
        d_attended_low,
        value_piece.reshape(score_count, HEADS, head_size),
        preferred_element_type=jnp.float32,
    )
    d_scores = (d_weights * weights * (1.0 - weights)).astype(jnp.bfloat16)
    weights, d_scores, key_heads = (
        weights,
        d_scores,
        key_piece.reshape(score_count, HEADS, head_size),
    )
    d_query = (
        jnp.einsum("hqk,khd->qhd", d_scores, key_heads, preferred_element_type=jnp.float32) * scale
    )
    key_term = (
        jnp.einsum("hqk,qhd->khd", d_scores, query_rot, preferred_element_type=jnp.float32) * scale
    )
    value_term = jnp.einsum(
        "hqk,qhd->khd",
        weights.astype(jnp.bfloat16),
        d_attended_low,
        preferred_element_type=jnp.float32,
    )
    d_keys = key_term.reshape(count, width)
    d_values = value_term.reshape(count, width)
    backward_sums = (d_query, d_keys, d_values)
    d_query = backward_sums[0]
    key_grad, value_grad = (
        lax.psum_scatter(
            backward_sums[1].astype(jnp.bfloat16), "seq", scatter_dimension=0, tiled=True
        ).astype(jnp.float32),
        lax.psum_scatter(
            backward_sums[2].astype(jnp.bfloat16), "seq", scatter_dimension=0, tiled=True
        ).astype(jnp.float32),
    )
    d_projected = jnp.concatenate(
        [
            unrotate(d_query, cosine, sine).reshape(rows, width),
            unrotate(key_grad.reshape(rows, HEADS, head_size), cosine, sine).reshape(rows, width),
            value_grad,
        ],
        axis=1,
    ).astype(jnp.bfloat16)
    d_attend_input = weights_back(d_projected, inner_weight)
    grad_inner = reduce_in(attend_input, d_projected)
    partial_gain_one = jnp.sum(d_attend_input * normed_first, axis=0)
    input_gradient = d_residual + norm_back(d_attend_input * gain_one, normed_first, inverse_first)
    local_squares = (
        jnp.sum(grad_inner * grad_inner)
        + jnp.sum(grad_outer * grad_outer)
        + jnp.sum(grad_expand * grad_expand)
    )
    local_squares = local_squares + jnp.sum(grad_shrink * grad_shrink)
    matrix_squares, gains_whole = lax.psum(
        (local_squares, jnp.stack([partial_gain_one, partial_gain_two])), ("dp", "seq")
    )
    owned_gains = norm_gains.shape[1]
    grad_gains = lax.dynamic_slice_in_dim(
        gains_whole, lax.axis_index(("dp", "seq")) * owned_gains, owned_gains, 1
    )
    global_norm = jnp.sqrt(matrix_squares + jnp.sum(gains_whole * gains_whole))
    factor = CLIP / jnp.maximum(global_norm, CLIP)
    gradients = (grad_inner, grad_outer, grad_expand, grad_shrink, grad_gains)
    masters = (inner_weight, outer_weight, expand_weight, shrink_weight, norm_gains)
    firsts = (first_inner, first_outer, first_expand, first_shrink, first_gains)
    seconds = (second_inner, second_outer, second_expand, second_shrink, second_gains)
    decays = (DECAY, DECAY, DECAY, DECAY, 0.0)
    rates = (RATE, RATE, RATE, RATE, GAIN_RATE)
    results = [
        adamw(
            masters[index],
            gradients[index],
            firsts[index],
            seconds[index],
            factor,
            decays[index],
            rates[index],
        )
        for index in range(5)
    ]
    return (
        output[None],
        input_gradient[None],
        global_norm,
        results[0][0],
        results[1][0],
        results[2][0],
        results[3][0],
        results[4][0],
        results[0][1],
        results[1][1],
        results[2][1],
        results[3][1],
        results[4][1],
        results[0][2],
        results[1][2],
        results[2][2],
        results[3][2],
        results[4][2],
    )


def solution(mesh):
    whole_heads = HEADS % mesh.shape["seq"] == 0 and mesh.shape["dp"] == 4
    placed = (
        P("dp", "seq", None),
        P("dp", "seq", None),
        P(("dp", "seq"), None),
        P(("dp", "seq"), None),
        P(("dp", "seq"), None),
        P(("dp", "seq"), None),
        P(None, ("dp", "seq")),
        P(("dp", "seq"), None),
        P(("dp", "seq"), None),
        P(("dp", "seq"), None),
        P(("dp", "seq"), None),
        P(None, ("dp", "seq")),
        P(("dp", "seq"), None),
        P(("dp", "seq"), None),
        P(("dp", "seq"), None),
        P(("dp", "seq"), None),
        P(None, ("dp", "seq")),
        P("dp", "seq"),
        P(),
    )
    return jax.shard_map(
        body if whole_heads else gathered_body,
        mesh=mesh,
        in_specs=placed,
        out_specs=(
            P("dp", "seq", None),
            P("dp", "seq", None),
            P(),
            P(("dp", "seq"), None),
            P(("dp", "seq"), None),
            P(("dp", "seq"), None),
            P(("dp", "seq"), None),
            P(None, ("dp", "seq")),
            P(("dp", "seq"), None),
            P(("dp", "seq"), None),
            P(("dp", "seq"), None),
            P(("dp", "seq"), None),
            P(None, ("dp", "seq")),
            P(("dp", "seq"), None),
            P(("dp", "seq"), None),
            P(("dp", "seq"), None),
            P(("dp", "seq"), None),
            P(None, ("dp", "seq")),
        ),
        check_vma=False,
    )
```

```python
import math

import jax
import jax.numpy as jnp
from jax import lax
from jax.experimental import pallas as pl
from jax.experimental.pallas import tpu as pltpu
from jax.sharding import PartitionSpec as P

HEADS = 16
STEP = 10


EPSILON = 1e-05
THETA = 10000.0
BETA_ONE = 0.9
BETA_TWO = 0.95
RATE = 0.05
GAIN_RATE = 0.5
DECAY = 0.1
ADAM_EPSILON = 1e-08
CLIP = 1.0
BOTH = ("dp", "seq")


def angles(positions, width):
    frequency = THETA ** (-(jnp.arange(width // 2, dtype=jnp.float32) * 2.0) / width)
    turned = positions.astype(jnp.float32)[:, None] * frequency[None, :]
    return (jnp.cos(turned)[:, None, :], jnp.sin(turned)[:, None, :])


def rotate(values, cosine, sine):
    half = values.shape[-1] // 2
    first, second = (values[..., :half], values[..., half:])
    return jnp.concatenate(
        [first * cosine - second * sine, second * cosine + first * sine], axis=-1
    )


def unrotate(upstream, cosine, sine):
    half = upstream.shape[-1] // 2
    first, second = (upstream[..., :half], upstream[..., half:])
    return jnp.concatenate(
        [first * cosine + second * sine, second * cosine - first * sine], axis=-1
    )


def norm_back(upstream, normed, inverse):
    return inverse * (upstream - normed * jnp.mean(upstream * normed, axis=-1, keepdims=True))


def contract_rows(left, right):
    return lax.dot_general(
        left, right, (((0,), (0,)), ((), ())), preferred_element_type=jnp.float32
    )


def contract_last(left, right):
    return lax.dot_general(
        left, right, (((1,), (1,)), ((), ())), preferred_element_type=jnp.float32
    )


def multiply(left, right):
    return jnp.dot(left, right, preferred_element_type=jnp.float32)


def adamw(weight, grad, first, second, factor, decay, rate):
    grad = grad * factor
    first = BETA_ONE * first + (1.0 - BETA_ONE) * grad
    second = BETA_TWO * second + (1.0 - BETA_TWO) * grad * grad
    update = (
        first / (1.0 - BETA_ONE**STEP) / (jnp.sqrt(second / (1.0 - BETA_TWO**STEP)) + ADAM_EPSILON)
    )
    return (first, second, weight - rate * (update + decay * weight))


def move(value, where):
    pairs = []
    for dp in range(lax.axis_size("dp")):
        for seq in range(lax.axis_size("seq")):
            target = where(dp, seq // 2, seq % 2)
            if target is not None:
                pairs.append(
                    (
                        dp * lax.axis_size("seq") + seq,
                        target[0] * lax.axis_size("seq") + target[1] * 2 + target[2],
                    )
                )
    return lax.ppermute(value, BOTH, pairs)


FAR_FIRST = [2, 3, 1, 0]
DEPTH = 4


def across(value):
    return move(value, lambda dp, z, x: (dp, z, 1 - x))


def turn(value, k):
    return move(value, lambda dp, z, x: (dp, z ^ k, x))


def line(value, hop, direction):
    def where(dp, z, x):
        if direction > 0:
            return (dp, z + 1, x) if z >= hop - 1 and z + 1 < DEPTH else None
        return (dp, z - 1, x) if z <= DEPTH - hop and z >= 1 else None

    return move(value, where)


def gather_rows(block, holds=()):
    z = lax.axis_index("seq") // 2
    up, down = [block], [block]
    for hop in range(1, DEPTH):
        held = holds[hop - 2 : hop - 1] if hop >= 2 else ()
        up.append(line(after(up[-1], *held), hop, 1))
        down.append(line(after(down[-1], *held), hop, -1))
    column = [
        block,
        jnp.where(z % 2 == 0, down[1], up[1]),
        jnp.where(z < 2, down[2], up[2]),
        jnp.where(z < 2, jnp.where(z == 0, down[3], down[1]), jnp.where(z == 3, up[3], up[1])),
    ]
    return [jnp.concatenate([piece, across(piece)], axis=0) for piece in column]


def nothing(*others):
    firsts = [lax.slice(other, (0,) * other.ndim, (1,) * other.ndim) for other in others]
    return sum(first.reshape(()).astype(jnp.float32) for first in firsts) * 0.0


def after(value, *others):
    return value + nothing(*others).astype(value.dtype) if others else value


def pairs_of():
    return [(k, j) for k in range(DEPTH) for j in range(2)]


def sources_of():
    z, x = lax.axis_index("seq") // 2, lax.axis_index("seq") % 2
    return [(z ^ k) * 2 + (x ^ j) for k, j in pairs_of()]


def exchange(blocks):
    return lax.all_to_all(blocks, "seq", 0, 0, tiled=True)


def exchange_small(blocks):
    return [
        move(block, lambda dp, z, x: (dp, z ^ k, x ^ j)) if (k, j) != (0, 0) else block
        for (k, j), block in zip(pairs_of(), blocks, strict=True)
    ]


def by_place(columns, n_seq):
    rows, groups, _, size = columns.shape
    return columns.transpose(2, 0, 1, 3).reshape(n_seq, rows, -1)


def copy_block(order, source, target):
    target[...] = source[...]


def pick(blocks, order):
    count, rows, columns = blocks.shape
    block = (1, rows, columns)
    return pl.pallas_call(
        copy_block,
        grid_spec=pltpu.PrefetchScalarGridSpec(
            num_scalar_prefetch=1,
            grid=(count,),
            in_specs=[pl.BlockSpec(block, lambda i, order: (order[i], 0, 0))],
            out_specs=pl.BlockSpec(block, lambda i, order: (i, 0, 0)),
        ),
        out_shape=jax.ShapeDtypeStruct(blocks.shape, blocks.dtype),
        compiler_params=pltpu.CompilerParams(vmem_limit_bytes=32 * 1024 * 1024),
        cost_estimate=pl.CostEstimate(flops=0, bytes_accessed=4 * blocks.size, transcendentals=0),
    )(order.astype(jnp.int32), blocks)


def in_place(received):
    return pick(jnp.stack(received), jnp.stack(sources_of()))


def side_by_side(received):
    count, (rows, columns) = len(received), received[0].shape
    return pl.pallas_call(
        copy_block,
        grid_spec=pltpu.PrefetchScalarGridSpec(
            num_scalar_prefetch=1,
            grid=(count,),
            in_specs=[pl.BlockSpec((None, rows, columns), lambda i, order: (order[i], 0, 0))],
            out_specs=pl.BlockSpec((rows, columns), lambda i, order: (0, i)),
        ),
        out_shape=jax.ShapeDtypeStruct((rows, count * columns), received[0].dtype),
        compiler_params=pltpu.CompilerParams(vmem_limit_bytes=32 * 1024 * 1024),
        cost_estimate=pl.CostEstimate(
            flops=0, bytes_accessed=4 * count * rows * columns, transcendentals=0
        ),
    )(jnp.stack(sources_of()).astype(jnp.int32), jnp.stack(received))


def scatter_rows(partial, order):
    sums, came = {}, []
    for n, k in enumerate(order):
        term = partial(k, came[n - 2 : n - 1] if n >= 2 else [])
        rows = term.shape[0] // 2
        came.append(across(term[rows:]))
        total = term[:rows].astype(jnp.float32) + came[-1].astype(jnp.float32)
        sums[k] = turn(total.astype(jnp.bfloat16), k).astype(jnp.float32) if k else total
    return sum(sums[k] for k in range(DEPTH)), came


def sum_everywhere(value):
    def of_four(where):
        others = [move(value, lambda dp, z, x: where(dp, z, x, mask)) for mask in (1, 2, 3)]
        return (value + others[0]) + (others[1] + others[2])

    value = of_four(lambda dp, z, x, mask: (dp ^ mask, z, x))
    value = of_four(lambda dp, z, x, mask: (dp, z ^ mask, x))
    return value + across(value)


def other_core(value):
    return move(value, lambda dp, z, x: (dp ^ 1, z, x))


def other_y(value):
    return move(value, lambda dp, z, x: (dp ^ 2, z, x))


def share(rows):
    return lax.all_gather(rows, "dp", axis=0, tiled=True)


def share_by_hand(rows):
    dp = lax.axis_index("dp")
    pair = jnp.stack([rows, other_y(rows)])
    other = other_core(pair)
    masks = [at ^ dp for at in range(4)]
    order = jnp.stack([(mask % 2) * 2 + mask // 2 for mask in masks])
    whole = pick(jnp.concatenate([pair, other]), order)
    return whole.reshape(-1, *rows.shape[1:]), pair[1]


def share_small(value):
    dp = lax.axis_index("dp")
    whole = jnp.zeros((4, *value.shape), value.dtype)
    for mask in range(4):
        piece = move(value, lambda dp, z, x: (dp ^ mask, z, x)) if mask else value
        whole = lax.dynamic_update_index_in_dim(whole, piece, dp ^ mask, 0)
    return whole


def reduce_over(rows):
    return lax.psum_scatter(rows, "dp", scatter_dimension=0, tiled=True)


def take(array, index, axis):
    return lax.dynamic_index_in_dim(array, index, axis, keepdims=False)


def add_low(left, right, *holds):
    total = left.astype(jnp.float32) + right.astype(jnp.float32)
    return after(total, *holds).astype(jnp.bfloat16)


def reduce_by_hand(rows, *holds):
    dp = lax.axis_index("dp")
    y, core = dp // 2, dp % 2
    parts = rows.reshape(2, 2, -1, *rows.shape[1:])
    parts = add_low(take(parts, core, 1), other_core(take(parts, 1 - core, 1)))
    return add_low(take(parts, y, 0), other_y(take(parts, 1 - y, 0)), *holds)


def reduce_along_seq(rows, holds, last_holds):
    z, x = lax.axis_index("seq") // 2, lax.axis_index("seq") % 2
    parts = rows.reshape(DEPTH, 2, -1, *rows.shape[1:])
    parts = add_low(take(parts, x, 1), across(take(parts, 1 - x, 1)), *holds)
    total = after(take(parts, z, 0).astype(jnp.float32), *last_holds)
    for k in range(1, DEPTH):
        total = total + turn(take(parts, z ^ k, 0), k).astype(jnp.float32)
    return total


def body(
    tokens,
    cotangent,
    inner_weight,
    outer_weight,
    expand_weight,
    shrink_weight,
    norm_gains,
    first_inner,
    first_outer,
    first_expand,
    first_shrink,
    first_gains,
    second_inner,
    second_outer,
    second_expand,
    second_shrink,
    second_gains,
    document_index,
    group_order,
):
    bf16, f32 = jnp.bfloat16, jnp.float32
    rows, width = tokens.shape[1:]
    n_dp, n_seq = lax.axis_size("dp"), lax.axis_size("seq")
    head = width // HEADS
    own_heads = HEADS // n_seq
    own_width = own_heads * head
    owned = inner_weight.shape[0]
    length = rows * n_seq
    scale = head ** (-0.5)
    offset = -math.log(length)
    group = rows // 2
    hidden = expand_weight.shape[1] // 2
    share_hidden = hidden // n_seq
    slab = shrink_weight.shape[0]
    device = lax.axis_index(BOTH)
    sources = sources_of()

    inputs_low = tokens[0]
    upstream = cotangent[0]

    with jax.named_scope("inner"):
        gain_parts = share_small(norm_gains.astype(bf16).reshape(-1))
        small = jnp.concatenate([gain_parts.reshape(-1), document_index[0].astype(bf16)])
        small = jnp.pad(small[None], ((0, 15), (0, 3 * own_width - small.size)))
        inner_low = by_place(inner_weight.astype(bf16).reshape(owned, 3, n_seq, own_width), n_seq)
        small = jnp.broadcast_to(small, (n_seq, *small.shape))
        inner_blocks = exchange(jnp.concatenate([inner_low, small], axis=1))
        inner, inner_first = share_by_hand(inner_blocks[:, :owned].reshape(n_seq * owned, -1))
        small = inner_blocks[:, owned]
        gains = small[:, : gain_parts.size].reshape(n_seq, n_dp, 2, -1).astype(f32)
        gains = gains.transpose(2, 1, 0, 3).reshape(2, width)
        documents = small[:, gain_parts.size : gain_parts.size + rows]
        documents = jnp.concatenate([take(documents, s, 0) for s in sources]).astype(f32)
    with jax.named_scope("shrink"):
        shrink = share(shrink_weight.astype(bf16))
    gain_one, gain_two = gains[0], gains[1]

    groups = jnp.concatenate([lax.dynamic_slice_in_dim(group_order, 2 * s, 2) for s in sources])
    within = jnp.arange(group, dtype=jnp.int32)
    places = (groups[:, None] * group + within[None, :]).reshape(-1)
    cosine, sine = (part[:, 0] for part in angles(places, head))
    cosine, sine = jnp.concatenate([cosine] * 2, axis=1), jnp.concatenate([-sine, sine], axis=1)

    def turned(values, sign):
        half = head // 2
        swapped = jnp.concatenate([values[:, half:], values[:, :half]], axis=1)
        return values * cosine + swapped * (sine * sign)

    def head_of(array, part, h):
        start = (part * own_heads + h) * head
        return array[:, start : start + head]

    def first_norm(piece):
        values = piece.astype(f32)
        inverse = lax.rsqrt(jnp.mean(values * values, axis=-1, keepdims=True) + EPSILON)
        return values * inverse, inverse

    with jax.named_scope("tokens"):
        block = jnp.concatenate([inputs_low, outer_weight.astype(bf16)], axis=0)
        pieces = gather_rows(block, [inner_blocks, inner_first])
        pieces = [piece.reshape(2, rows + owned, width) for piece in pieces]
        token_pieces = [piece[:, :rows].reshape(2 * rows, width) for piece in pieces]
    with jax.named_scope("outer"):
        outer = [piece[j, rows:] for piece in pieces for j in range(2)]
        outer[0] = after(outer[0], shrink)
        outer = share(in_place(outer).reshape(n_seq * owned, width))
    with jax.named_scope("expand"):
        expand_low = after(expand_weight, *token_pieces[1:]).astype(bf16)
        expand_low = expand_low.reshape(owned, 2 * n_dp, n_seq, slab)
        expand_blocks = exchange(by_place(expand_low, n_seq))
    with jax.named_scope("attend"):
        attend_pieces = [(first_norm(piece)[0] * gain_one).astype(bf16) for piece in token_pieces]
        projected = jnp.concatenate([multiply(piece, inner) for piece in attend_pieces], axis=0)
        visible = (documents[:, None] == documents[None, :]) & (places[None, :] <= places[:, None])
        visible = visible.astype(f32)
        query_rot, key_rot, value_low, weights, attended = [], [], [], [], []
        for h in range(own_heads):
            query_rot.append(turned(head_of(projected, 0, h), 1.0).astype(bf16))
            key_rot.append(turned(head_of(projected, 1, h), 1.0).astype(bf16))
            value_low.append(head_of(projected, 2, h).astype(bf16))
            scores = contract_last(query_rot[h], key_rot[h]) * scale + offset
            weights.append(jax.nn.sigmoid(scores) * visible)
            attended.append(multiply(weights[h].astype(bf16), value_low[h]).astype(bf16))
        attended = jnp.concatenate(attended, axis=1).reshape(n_seq, rows, own_width)

    with jax.named_scope("rows"):
        attended_rows = side_by_side(exchange_small(list(attended)))
    with jax.named_scope("expand"):
        expand_blocks = after(expand_blocks, attended_rows, outer)
        expand = share(expand_blocks.reshape(n_seq * owned, -1))
    inputs = inputs_low.astype(f32)
    residual = inputs + multiply(attended_rows, outer)
    inverse_second = lax.rsqrt(jnp.mean(residual * residual, axis=-1, keepdims=True) + EPSILON)
    normed_second = residual * inverse_second

    with jax.named_scope("mlp_input"):
        mlp_pieces = gather_rows((normed_second * gain_two).astype(bf16))
    with jax.named_scope("gate_up"):
        gate_ups = [multiply(piece, expand) for piece in mlp_pieces]
    with jax.named_scope("cotangent"):
        upstream_pieces = gather_rows(after(upstream, *mlp_pieces[1:]))
    activations, gate_up_grads = [None] * DEPTH, [None] * DEPTH

    def feed_back(k, earlier):
        gate, upward = gate_ups[k][:, :share_hidden], gate_ups[k][:, share_hidden:]
        gate = after(gate, *earlier)
        squash = jax.nn.sigmoid(gate)
        activations[k] = (gate * squash * upward).astype(bf16)
        down_grad = contract_last(upstream_pieces[k], shrink)
        d_gate = down_grad * upward * squash * (1.0 + gate * (1.0 - squash))
        d_upward = down_grad * gate * squash
        gate_up_grads[k] = jnp.concatenate([d_gate, d_upward], axis=1).astype(bf16)
        return contract_last(gate_up_grads[k], expand).astype(bf16)

    with jax.named_scope("d_mlp_input"):
        d_mlp_input, came = scatter_rows(feed_back, [0, 2, 1, 3])
    with jax.named_scope("grad_expand"):
        grad_expand = contract_rows(
            jnp.concatenate(mlp_pieces, axis=0), jnp.concatenate(gate_up_grads, axis=0)
        )
        grad_expand = after(grad_expand, *came[3:4]).astype(bf16)
    with jax.named_scope("grad_shrink"):
        grad_shrink = contract_rows(
            jnp.concatenate(activations, axis=0), jnp.concatenate(upstream_pieces, axis=0)
        )
        grad_shrink = after(grad_shrink, *came[3:4]).astype(bf16)
    d_mlp_input = after(d_mlp_input, grad_expand, grad_shrink)
    with jax.named_scope("grad_expand"):
        grad_expand = reduce_over(grad_expand)
    with jax.named_scope("grad_shrink"):
        grad_shrink = reduce_over(grad_shrink).astype(f32)
    partial_gain_two = jnp.sum(d_mlp_input * normed_second, axis=0)
    d_residual = upstream.astype(f32) + norm_back(
        d_mlp_input * gain_two, normed_second, inverse_second
    )

    with jax.named_scope("heads"):
        d_residual_low = d_residual.astype(bf16)
        d_attended = contract_last(d_residual_low, outer).astype(bf16)
        d_attended = by_place(d_attended.reshape(rows, 1, n_seq, own_width), n_seq)
        d_attended = exchange_small([take(d_attended, s, 0) for s in sources])
        d_attended = jnp.concatenate(d_attended)
    with jax.named_scope("attend_back"):
        d_query, d_key, d_value = [], [], []
        for h in range(own_heads):
            d_out = head_of(d_attended, 0, h)
            d_weights = contract_last(d_out, value_low[h])
            d_scores = (d_weights * weights[h] * (1.0 - weights[h])).astype(bf16)
            d_query.append(turned(multiply(d_scores, key_rot[h]) * scale, -1.0))
            d_key.append(turned(contract_rows(d_scores, query_rot[h]) * scale, -1.0))
            d_value.append(contract_rows(weights[h].astype(bf16), d_out))
        d_projected = jnp.concatenate(
            [part.astype(bf16) for part in d_query + d_key + d_value], axis=1
        )
    with jax.named_scope("feed"):
        feed = multiply(jnp.concatenate(activations, axis=0), shrink)
        feed = after(feed, d_attended).astype(bf16).reshape(DEPTH, 2, rows, width)
        feed = add_low(feed[:, 0], across(feed[:, 1]), d_projected)
        output = residual + feed[0].astype(f32)
        for k in range(1, DEPTH):
            output = output + turn(feed[k], k).astype(f32)
    gain_terms = [None] * DEPTH

    def attend_back(k, earlier):
        term = contract_last(d_projected[2 * rows * k : 2 * rows * (k + 1)], inner)
        if k == FAR_FIRST[0]:
            term = after(term, feed)
        gain_terms[k] = jnp.sum(term * first_norm(token_pieces[k])[0], axis=0)
        return term.astype(bf16)

    with jax.named_scope("d_attend_input"):
        d_attend_input, came_last = scatter_rows(attend_back, FAR_FIRST)
    partial_gain_one = sum(gain_terms)
    normed_first, inverse_first = first_norm(inputs_low)
    input_gradient = d_residual + norm_back(d_attend_input * gain_one, normed_first, inverse_first)

    with jax.named_scope("own_expand"):
        own_expand = exchange(grad_expand.reshape(n_seq, owned, -1))
    with jax.named_scope("grad_outer"):
        grad_outer = contract_rows(attended_rows, d_residual_low).astype(bf16)
        grad_outer = reduce_by_hand(grad_outer, came_last[-1])
        grad_outer = reduce_along_seq(grad_outer, [d_attend_input], [own_expand])
    grad_inner = contract_rows(jnp.concatenate(attend_pieces, axis=0), d_projected)
    with jax.named_scope("grad_inner"):
        grad_inner = reduce_by_hand(grad_inner.astype(bf16), came_last[-1])

    local_squares = sum(
        jnp.sum(jnp.square(grad.astype(f32)))
        for grad in (grad_inner, grad_outer, grad_expand, grad_shrink)
    )
    with jax.named_scope("sums"):
        sums = sum_everywhere(
            jnp.concatenate(
                [partial_gain_one, partial_gain_two, jnp.full((128,), local_squares)]
            ).reshape(-1, 128)
        ).reshape(-1)
    gains_whole = sums[: 2 * width].reshape(2, width)
    grad_gains = lax.dynamic_slice_in_dim(
        gains_whole, device * norm_gains.shape[1], norm_gains.shape[1], 1
    )
    global_norm = jnp.sqrt(sums[2 * width] + jnp.sum(gains_whole * gains_whole))
    factor = CLIP / jnp.maximum(global_norm, CLIP)

    with jax.named_scope("own_inner"):
        grad_inner = exchange(grad_inner.reshape(n_seq, owned, -1))
    grad_inner = grad_inner.reshape(n_seq, owned, 3, own_width)
    grad_inner = grad_inner.transpose(1, 2, 0, 3).reshape(inner_weight.shape)
    grad_expand = own_expand.reshape(n_seq, owned, 2 * n_dp, slab)
    grad_expand = grad_expand.transpose(1, 2, 0, 3).reshape(expand_weight.shape)

    gradients = (grad_inner, grad_outer, grad_expand, grad_shrink, grad_gains)
    masters = (inner_weight, outer_weight, expand_weight, shrink_weight, norm_gains)
    firsts = (first_inner, first_outer, first_expand, first_shrink, first_gains)
    seconds = (second_inner, second_outer, second_expand, second_shrink, second_gains)
    decays = (DECAY, DECAY, DECAY, DECAY, 0.0)
    rates = (RATE, RATE, RATE, RATE, GAIN_RATE)
    results = [
        adamw(
            masters[index],
            gradients[index].astype(f32),
            firsts[index],
            seconds[index],
            factor,
            decays[index],
            rates[index],
        )
        for index in range(5)
    ]
    return (
        output[None],
        input_gradient[None],
        global_norm,
        *(result[0] for result in results),
        *(result[1] for result in results),
        *(result[2] for result in results),
    )


def project_in(normed, weight, gain):
    rows = normed.shape[0]

    def add_piece(carry, pieces, start):
        piece_left = (normed * pieces[1].astype(jnp.float32)).astype(jnp.bfloat16)
        partial_sum = jnp.dot(piece_left, pieces[0], preferred_element_type=jnp.float32)
        return (partial_sum, pieces[1])

    initial = (
        jnp.zeros((rows, weight.shape[1]), jnp.float32),
        jnp.zeros((normed.shape[1],), jnp.bfloat16),
    )
    product, full_gain = add_piece(
        initial,
        (
            lax.all_gather(weight.astype(jnp.bfloat16), ("dp", "seq"), axis=0, tiled=True),
            lax.all_gather(gain.astype(jnp.bfloat16), ("dp", "seq"), axis=0, tiled=True),
        ),
        jnp.int32(0),
    )
    left = (normed * full_gain.astype(jnp.float32)).astype(jnp.bfloat16)
    return (product, left, None, full_gain.astype(jnp.float32))


def project_mid(left, weight):

    def add_piece(partial_sum, piece, start):
        return jnp.dot(left, piece, preferred_element_type=jnp.float32)

    initial = jnp.zeros((left.shape[0], weight.shape[1]), jnp.float32)
    product = add_piece(
        initial,
        lax.all_gather(weight.astype(jnp.bfloat16), ("dp", "seq"), axis=0, tiled=True),
        jnp.int32(0),
    )
    return (product, None)


def weights_back(upstream, weight):
    return contract_last(
        upstream, lax.all_gather(weight.astype(jnp.bfloat16), ("dp", "seq"), axis=0, tiled=True)
    )


def reduce_in(left, upstream):
    owned = left.shape[1] // lax.axis_size(("dp", "seq"))

    def term(start, count):
        return contract_rows(left, upstream)

    return lax.psum_scatter(
        term(jnp.int32(0), lax.axis_size(("dp", "seq")) * owned),
        ("dp", "seq"),
        scatter_dimension=0,
        tiled=True,
    )


def reduce_mid(left, upstream):
    owned = left.shape[1] // lax.axis_size(("dp", "seq"))

    def term(start, count):
        return contract_rows(left, upstream)

    return lax.psum_scatter(
        term(jnp.int32(0), lax.axis_size(("dp", "seq")) * owned),
        ("dp", "seq"),
        scatter_dimension=0,
        tiled=True,
    )


def gathered_body(
    tokens,
    cotangent,
    inner_weight,
    outer_weight,
    expand_weight,
    shrink_weight,
    norm_gains,
    first_inner,
    first_outer,
    first_expand,
    first_shrink,
    first_gains,
    second_inner,
    second_outer,
    second_expand,
    second_shrink,
    second_gains,
    document_index,
    group_order,
):
    inputs = tokens[0].astype(jnp.float32)
    rows, width = inputs.shape
    head_size = width // HEADS
    length = rows * lax.axis_size("seq")
    scale = head_size ** (-0.5)
    offset = -math.log(length)
    group = rows // 2
    within = jnp.arange(group, dtype=jnp.int32)
    paired = lax.dynamic_slice_in_dim(group_order, 2 * lax.axis_index("seq"), 2)
    own_place = (paired[:, None] * group + within[None, :]).reshape(-1)
    all_places = (group_order[:, None] * group + within[None, :]).reshape(-1)
    own_document = document_index[0].astype(jnp.bfloat16)
    cosine, sine = angles(own_place, head_size)
    inverse_first = lax.rsqrt(jnp.mean(inputs * inputs, axis=-1, keepdims=True) + EPSILON)
    normed_first = inputs * inverse_first
    projected, attend_input, kept_inner, gain_one = project_in(
        normed_first, inner_weight, norm_gains[0]
    )
    queries = projected[:, :width].reshape(rows, HEADS, head_size)
    query_rot = rotate(queries, cosine, sine).astype(jnp.bfloat16)
    key_rot = rotate(projected[:, width : 2 * width].reshape(rows, HEADS, head_size), cosine, sine)
    key_rot = key_rot.reshape(rows, width).astype(jnp.bfloat16)
    value_low = projected[:, 2 * width :].astype(jnp.bfloat16)

    def sigmoid_weights(key_piece, document_piece):
        count = key_piece.shape[0]
        scores = (
            jnp.einsum(
                "qhd,khd->hqk",
                query_rot,
                key_piece.reshape(count, HEADS, head_size),
                preferred_element_type=jnp.float32,
            )
            * scale
            + offset
        )
        visible = (own_document[:, None] == document_piece[None, :]) & (
            all_places[None, :] <= own_place[:, None]
        )
        return jax.nn.sigmoid(scores) * visible.astype(jnp.float32)[None]

    key_piece = lax.all_gather(key_rot, "seq", axis=0, tiled=True)
    value_piece = lax.all_gather(value_low, "seq", axis=0, tiled=True)
    document_piece = lax.all_gather(own_document, "seq", axis=0, tiled=True)
    count = key_piece.shape[0]
    weights = sigmoid_weights(key_piece, document_piece).astype(jnp.bfloat16)
    attended = jnp.einsum(
        "hqk,khd->qhd",
        weights,
        value_piece.reshape(count, HEADS, head_size),
        preferred_element_type=jnp.float32,
    )
    attended = attended.reshape(rows, width).astype(jnp.bfloat16)
    branch, kept_outer = project_mid(attended, outer_weight)
    residual = inputs + branch
    inverse_second = lax.rsqrt(jnp.mean(residual * residual, axis=-1, keepdims=True) + EPSILON)
    normed_second = residual * inverse_second
    gate_up, mlp_input, kept_expand, gain_two = project_in(
        normed_second, expand_weight, norm_gains[1]
    )
    hidden = gate_up.shape[1] // 2
    gate = gate_up[:, :hidden]
    upward = gate_up[:, hidden:]
    squash = jax.nn.sigmoid(gate)
    activation = (gate * squash * upward).astype(jnp.bfloat16)
    feed, kept_shrink = project_mid(activation, shrink_weight)
    output = residual + feed
    upstream = cotangent[0]
    down_grad = weights_back(upstream, shrink_weight)
    grad_shrink = reduce_mid(activation, upstream)
    d_gate = down_grad * upward * squash * (1.0 + gate * (1.0 - squash))
    d_upward = down_grad * gate * squash
    d_gate_up = jnp.concatenate([d_gate, d_upward], axis=1).astype(jnp.bfloat16)
    d_mlp_input = weights_back(d_gate_up, expand_weight)
    grad_expand = reduce_in(mlp_input, d_gate_up)
    partial_gain_two = jnp.sum(d_mlp_input * normed_second, axis=0)
    d_residual = upstream.astype(jnp.float32) + norm_back(
        d_mlp_input * gain_two, normed_second, inverse_second
    )
    d_residual_low = d_residual.astype(jnp.bfloat16)
    d_attended = weights_back(d_residual_low, outer_weight)
    grad_outer = reduce_mid(attended, d_residual_low)
    d_attended_flat = d_attended.astype(jnp.bfloat16)
    d_attended_low = d_attended_flat.reshape(rows, HEADS, head_size)
    key_piece = lax.all_gather(key_rot, "seq", axis=0, tiled=True)
    value_piece = lax.all_gather(value_low, "seq", axis=0, tiled=True)
    document_piece = lax.all_gather(own_document, "seq", axis=0, tiled=True)
    count = key_piece.shape[0]
    score_count = key_piece.shape[0]
    weights = sigmoid_weights(key_piece, document_piece)
    d_weights = jnp.einsum(
        "qhd,khd->hqk",
        d_attended_low,
        value_piece.reshape(score_count, HEADS, head_size),
        preferred_element_type=jnp.float32,
    )
    d_scores = (d_weights * weights * (1.0 - weights)).astype(jnp.bfloat16)
    weights, d_scores, key_heads = (
        weights,
        d_scores,
        key_piece.reshape(score_count, HEADS, head_size),
    )
    d_query = (
        jnp.einsum("hqk,khd->qhd", d_scores, key_heads, preferred_element_type=jnp.float32) * scale
    )
    key_term = (
        jnp.einsum("hqk,qhd->khd", d_scores, query_rot, preferred_element_type=jnp.float32) * scale
    )
    value_term = jnp.einsum(
        "hqk,qhd->khd",
        weights.astype(jnp.bfloat16),
        d_attended_low,
        preferred_element_type=jnp.float32,
    )
    d_keys = key_term.reshape(count, width)
    d_values = value_term.reshape(count, width)
    backward_sums = (d_query, d_keys, d_values)
    d_query = backward_sums[0]
    key_grad, value_grad = (
        lax.psum_scatter(
            backward_sums[1].astype(jnp.bfloat16), "seq", scatter_dimension=0, tiled=True
        ).astype(jnp.float32),
        lax.psum_scatter(
            backward_sums[2].astype(jnp.bfloat16), "seq", scatter_dimension=0, tiled=True
        ).astype(jnp.float32),
    )
    d_projected = jnp.concatenate(
        [
            unrotate(d_query, cosine, sine).reshape(rows, width),
            unrotate(key_grad.reshape(rows, HEADS, head_size), cosine, sine).reshape(rows, width),
            value_grad,
        ],
        axis=1,
    ).astype(jnp.bfloat16)
    d_attend_input = weights_back(d_projected, inner_weight)
    grad_inner = reduce_in(attend_input, d_projected)
    partial_gain_one = jnp.sum(d_attend_input * normed_first, axis=0)
    input_gradient = d_residual + norm_back(d_attend_input * gain_one, normed_first, inverse_first)
    local_squares = (
        jnp.sum(grad_inner * grad_inner)
        + jnp.sum(grad_outer * grad_outer)
        + jnp.sum(grad_expand * grad_expand)
    )
    local_squares = local_squares + jnp.sum(grad_shrink * grad_shrink)
    matrix_squares, gains_whole = lax.psum(
        (local_squares, jnp.stack([partial_gain_one, partial_gain_two])), ("dp", "seq")
    )
    owned_gains = norm_gains.shape[1]
    grad_gains = lax.dynamic_slice_in_dim(
        gains_whole, lax.axis_index(("dp", "seq")) * owned_gains, owned_gains, 1
    )
    global_norm = jnp.sqrt(matrix_squares + jnp.sum(gains_whole * gains_whole))
    factor = CLIP / jnp.maximum(global_norm, CLIP)
    gradients = (grad_inner, grad_outer, grad_expand, grad_shrink, grad_gains)
    masters = (inner_weight, outer_weight, expand_weight, shrink_weight, norm_gains)
    firsts = (first_inner, first_outer, first_expand, first_shrink, first_gains)
    seconds = (second_inner, second_outer, second_expand, second_shrink, second_gains)
    decays = (DECAY, DECAY, DECAY, DECAY, 0.0)
    rates = (RATE, RATE, RATE, RATE, GAIN_RATE)
    results = [
        adamw(
            masters[index],
            gradients[index],
            firsts[index],
            seconds[index],
            factor,
            decays[index],
            rates[index],
        )
        for index in range(5)
    ]
    return (
        output[None],
        input_gradient[None],
        global_norm,
        results[0][0],
        results[1][0],
        results[2][0],
        results[3][0],
        results[4][0],
        results[0][1],
        results[1][1],
        results[2][1],
        results[3][1],
        results[4][1],
        results[0][2],
        results[1][2],
        results[2][2],
        results[3][2],
        results[4][2],
    )


def solution(mesh):
    whole_heads = mesh.shape["seq"] == 2 * DEPTH and mesh.shape["dp"] == 4
    placed = (
        P("dp", "seq", None),
        P("dp", "seq", None),
        P(("dp", "seq"), None),
        P(("dp", "seq"), None),
        P(("dp", "seq"), None),
        P(("dp", "seq"), None),
        P(None, ("dp", "seq")),
        P(("dp", "seq"), None),
        P(("dp", "seq"), None),
        P(("dp", "seq"), None),
        P(("dp", "seq"), None),
        P(None, ("dp", "seq")),
        P(("dp", "seq"), None),
        P(("dp", "seq"), None),
        P(("dp", "seq"), None),
        P(("dp", "seq"), None),
        P(None, ("dp", "seq")),
        P("dp", "seq"),
        P(),
    )
    return jax.shard_map(
        body if whole_heads else gathered_body,
        mesh=mesh,
        in_specs=placed,
        out_specs=(
            P("dp", "seq", None),
            P("dp", "seq", None),
            P(),
            P(("dp", "seq"), None),
            P(("dp", "seq"), None),
            P(("dp", "seq"), None),
            P(("dp", "seq"), None),
            P(None, ("dp", "seq")),
            P(("dp", "seq"), None),
            P(("dp", "seq"), None),
            P(("dp", "seq"), None),
            P(("dp", "seq"), None),
            P(None, ("dp", "seq")),
            P(("dp", "seq"), None),
            P(("dp", "seq"), None),
            P(("dp", "seq"), None),
            P(("dp", "seq"), None),
            P(None, ("dp", "seq")),
        ),
        check_vma=False,
    )
```

```python
import math

import jax
import jax.numpy as jnp
from jax import lax
from jax.experimental import pallas as pl
from jax.experimental.pallas import tpu as pltpu
from jax.sharding import PartitionSpec as P

HEADS = 16
STEP = 10


EPSILON = 1e-05
THETA = 10000.0
BETA_ONE = 0.9
BETA_TWO = 0.95
RATE = 0.05
GAIN_RATE = 0.5
DECAY = 0.1
ADAM_EPSILON = 1e-08
CLIP = 1.0
BOTH = ("dp", "seq")


def angles(positions, width):
    frequency = THETA ** (-(jnp.arange(width // 2, dtype=jnp.float32) * 2.0) / width)
    turned = positions.astype(jnp.float32)[:, None] * frequency[None, :]
    return (jnp.cos(turned)[:, None, :], jnp.sin(turned)[:, None, :])


def rotate(values, cosine, sine):
    half = values.shape[-1] // 2
    first, second = (values[..., :half], values[..., half:])
    return jnp.concatenate(
        [first * cosine - second * sine, second * cosine + first * sine], axis=-1
    )


def unrotate(upstream, cosine, sine):
    half = upstream.shape[-1] // 2
    first, second = (upstream[..., :half], upstream[..., half:])
    return jnp.concatenate(
        [first * cosine + second * sine, second * cosine - first * sine], axis=-1
    )


def norm_back(upstream, normed, inverse):
    return inverse * (upstream - normed * jnp.mean(upstream * normed, axis=-1, keepdims=True))


def contract_rows(left, right):
    return lax.dot_general(
        left, right, (((0,), (0,)), ((), ())), preferred_element_type=jnp.float32
    )


def contract_last(left, right):
    return lax.dot_general(
        left, right, (((1,), (1,)), ((), ())), preferred_element_type=jnp.float32
    )


def multiply(left, right):
    return jnp.dot(left, right, preferred_element_type=jnp.float32)


def adamw(weight, grad, first, second, factor, decay, rate):
    grad = grad * factor
    first = BETA_ONE * first + (1.0 - BETA_ONE) * grad
    second = BETA_TWO * second + (1.0 - BETA_TWO) * grad * grad
    update = (
        first / (1.0 - BETA_ONE**STEP) / (jnp.sqrt(second / (1.0 - BETA_TWO**STEP)) + ADAM_EPSILON)
    )
    return (first, second, weight - rate * (update + decay * weight))


def adamw_blocks(factor, weight, grad, first, second, weight_new, first_new, second_new):
    count = grad.shape[0] if len(grad.shape) == 3 else 1
    size = weight.shape[1] // count
    for index in range(count):
        columns = pl.ds(index * size, size)
        low = grad[index] if len(grad.shape) == 3 else grad[...]
        result = adamw(
            weight[:, columns],
            low.astype(jnp.float32),
            first[:, columns],
            second[:, columns],
            factor[0],
            DECAY,
            RATE,
        )
        first_new[:, columns], second_new[:, columns], weight_new[:, columns] = result


def adamw_matrix(weight, grad, first, second, factor, size=0):
    rows, columns = weight.shape
    if grad.ndim == 3:
        places = grad.shape[0]
        grad_spec = pl.BlockSpec((places, rows, size), lambda i: (0, 0, i))
        grid = (grad.shape[2] // size,)
        spec = pl.BlockSpec((rows, places * size), lambda i: (0, i))
    else:
        grid = (rows // 64,)
        spec = grad_spec = pl.BlockSpec((64, columns), lambda i: (i, 0))
    result = jax.ShapeDtypeStruct(weight.shape, jnp.float32)
    weight_new, first_new, second_new = pl.pallas_call(
        adamw_blocks,
        grid=grid,
        in_specs=[pl.BlockSpec(memory_space=pltpu.SMEM), spec, grad_spec, spec, spec],
        out_specs=[spec, spec, spec],
        out_shape=[result, result, result],
        compiler_params=pltpu.CompilerParams(vmem_limit_bytes=56 * 1024 * 1024),
        cost_estimate=pl.CostEstimate(
            flops=20 * weight.size, bytes_accessed=26 * weight.size, transcendentals=weight.size
        ),
    )(factor.reshape(1), weight, grad, first, second)
    return first_new, second_new, weight_new


def move(value, where):
    pairs = []
    for dp in range(lax.axis_size("dp")):
        for seq in range(lax.axis_size("seq")):
            target = where(dp, seq // 2, seq % 2)
            if target is not None:
                pairs.append(
                    (
                        dp * lax.axis_size("seq") + seq,
                        target[0] * lax.axis_size("seq") + target[1] * 2 + target[2],
                    )
                )
    return lax.ppermute(value, BOTH, pairs)


FAR_FIRST = [2, 3, 1, 0]
DEPTH = 4


def across(value):
    return move(value, lambda dp, z, x: (dp, z, 1 - x))


def turn(value, k):
    return move(value, lambda dp, z, x: (dp, z ^ k, x))


def line(value, hop, direction):
    def where(dp, z, x):
        if direction > 0:
            return (dp, z + 1, x) if z >= hop - 1 and z + 1 < DEPTH else None
        return (dp, z - 1, x) if z <= DEPTH - hop and z >= 1 else None

    return move(value, where)


def gather_rows(block, first_holds=(), last_holds=(), crossing=None):
    z = lax.axis_index("seq") // 2
    column, other = [block], [across(block)]

    def came(piece, *holds):
        column.append(after(piece, other[-1], *holds))
        other.append(across(column[-1]))

    up, down = line(block, 1, 1), line(block, 1, -1)
    up_one, down_one = up, down
    came(jnp.where(z % 2 == 0, down, up))
    up, down = line(after(up, *first_holds), 2, 1), line(after(down, *first_holds), 2, -1)
    came(jnp.where(z < 2, down, up))
    last_holds = (other[1], *last_holds)
    up, down = line(after(up, *last_holds), 3, 1), line(after(down, *last_holds), 3, -1)
    last = jnp.where(z < 2, jnp.where(z == 0, down, down_one), jnp.where(z == 3, up, up_one))
    came(last, *(crossing(last) if crossing else ()))
    return [jnp.concatenate(pair, axis=0) for pair in zip(column, other, strict=True)], column[-1]


def nothing(*others):
    firsts = [lax.slice(other, (0,) * other.ndim, (1,) * other.ndim) for other in others]
    return sum(first.reshape(()).astype(jnp.float32) for first in firsts) * 0.0


def after(value, *others):
    return value + nothing(*others).astype(value.dtype) if others else value


def after_in_place(value, *others):
    value = lax.optimization_barrier(value)
    start = (0,) * value.ndim
    first = lax.slice(value, start, (1,) * (value.ndim - 1) + (128,))
    return lax.dynamic_update_slice(value, after(first, *others), start)


def pairs_of():
    return [(k, j) for k in range(DEPTH) for j in range(2)]


def sources_of():
    z, x = lax.axis_index("seq") // 2, lax.axis_index("seq") % 2
    return [(z ^ k) * 2 + (x ^ j) for k, j in pairs_of()]


def exchange(blocks):
    return lax.all_to_all(blocks, "seq", 0, 0, tiled=True)


def exchange_small(blocks):
    return [
        move(block, lambda dp, z, x: (dp, z ^ k, x ^ j)) if (k, j) != (0, 0) else block
        for (k, j), block in zip(pairs_of(), blocks, strict=True)
    ]


def by_place(columns, n_seq):
    rows, groups, _, size = columns.shape
    return columns.transpose(2, 0, 1, 3).reshape(n_seq, rows, -1)


def copy_block(order, source, target):
    target[...] = source[...]


def pick(blocks, order):
    count, rows, columns = blocks.shape
    block = (1, rows, columns)
    return pl.pallas_call(
        copy_block,
        grid_spec=pltpu.PrefetchScalarGridSpec(
            num_scalar_prefetch=1,
            grid=(count,),
            in_specs=[pl.BlockSpec(block, lambda i, order: (order[i], 0, 0))],
            out_specs=pl.BlockSpec(block, lambda i, order: (i, 0, 0)),
        ),
        out_shape=jax.ShapeDtypeStruct(blocks.shape, blocks.dtype),
        compiler_params=pltpu.CompilerParams(vmem_limit_bytes=56 * 1024 * 1024),
        cost_estimate=pl.CostEstimate(flops=0, bytes_accessed=4 * blocks.size, transcendentals=0),
    )(order.astype(jnp.int32), blocks)


def in_place(received):
    return pick(jnp.stack(received), jnp.stack(sources_of()))


def side_by_side(received):
    count, (rows, columns) = len(received), received[0].shape
    return pl.pallas_call(
        copy_block,
        grid_spec=pltpu.PrefetchScalarGridSpec(
            num_scalar_prefetch=1,
            grid=(count,),
            in_specs=[pl.BlockSpec((None, rows, columns), lambda i, order: (order[i], 0, 0))],
            out_specs=pl.BlockSpec((rows, columns), lambda i, order: (0, i)),
        ),
        out_shape=jax.ShapeDtypeStruct((rows, count * columns), received[0].dtype),
        compiler_params=pltpu.CompilerParams(vmem_limit_bytes=56 * 1024 * 1024),
        cost_estimate=pl.CostEstimate(
            flops=0, bytes_accessed=4 * count * rows * columns, transcendentals=0
        ),
    )(jnp.stack(sources_of()).astype(jnp.int32), jnp.stack(received))


def scatter_rows(partial, order):
    sums, came = {}, []
    for n, k in enumerate(order):
        earlier = came[n - 2 : n - 1] if n >= 2 else []
        if n == DEPTH - 1:
            earlier = earlier + [sums[order[0]]] if order[0] else earlier
        term = partial(k, earlier)
        rows = term.shape[0] // 2
        came.append(across(term[rows:]))
        total = term[:rows].astype(jnp.float32) + came[-1].astype(jnp.float32)
        sums[k] = turn(total.astype(jnp.bfloat16), k) if k else total
    return sum(sums[k].astype(jnp.float32) for k in range(DEPTH)), came


def sum_everywhere(value):
    def of_four(where):
        others = [move(value, lambda dp, z, x: where(dp, z, x, mask)) for mask in (1, 2, 3)]
        return (value + others[0]) + (others[1] + others[2])

    value = of_four(lambda dp, z, x, mask: (dp ^ mask, z, x))
    value = of_four(lambda dp, z, x, mask: (dp, z ^ mask, x))
    return value + across(value)


def other_core(value):
    return move(value, lambda dp, z, x: (dp ^ 1, z, x))


def other_y(value):
    return move(value, lambda dp, z, x: (dp ^ 2, z, x))


def share(rows):
    return lax.all_gather(rows, "dp", axis=0, tiled=True)


def share_by_hand(rows):
    dp = lax.axis_index("dp")
    pair = jnp.stack([rows, other_y(rows)])
    other = other_core(pair)
    masks = [at ^ dp for at in range(4)]
    order = jnp.stack([(mask % 2) * 2 + mask // 2 for mask in masks])
    whole = pick(jnp.concatenate([pair, other]), order)
    return whole.reshape(-1, *rows.shape[1:]), pair[1]


def share_small(value):
    dp = lax.axis_index("dp")
    whole = jnp.zeros((4, *value.shape), value.dtype)
    for mask in range(4):
        piece = move(value, lambda dp, z, x: (dp ^ mask, z, x)) if mask else value
        whole = lax.dynamic_update_index_in_dim(whole, piece, dp ^ mask, 0)
    return whole


def reduce_over(rows):
    return lax.psum_scatter(rows, "dp", scatter_dimension=0, tiled=True)


def take(array, index, axis):
    return lax.dynamic_index_in_dim(array, index, axis, keepdims=False)


def add_low(left, right, *holds):
    total = left.astype(jnp.float32) + right.astype(jnp.float32)
    return after(total, *holds).astype(jnp.bfloat16)


def reduce_over_cores(rows):
    core = lax.axis_index("dp") % 2
    parts = rows.reshape(2, 2, -1, *rows.shape[1:])
    return add_low(take(parts, core, 1), other_core(take(parts, 1 - core, 1)))


def reduce_over_y(parts):
    y = lax.axis_index("dp") // 2
    return add_low(take(parts, y, 0), other_y(take(parts, 1 - y, 0)))


def body(
    tokens,
    cotangent,
    inner_weight,
    outer_weight,
    expand_weight,
    shrink_weight,
    norm_gains,
    first_inner,
    first_outer,
    first_expand,
    first_shrink,
    first_gains,
    second_inner,
    second_outer,
    second_expand,
    second_shrink,
    second_gains,
    document_index,
    group_order,
):
    bf16, f32 = jnp.bfloat16, jnp.float32
    rows, width = tokens.shape[1:]
    n_dp, n_seq = lax.axis_size("dp"), lax.axis_size("seq")
    head = width // HEADS
    own_heads = HEADS // n_seq
    own_width = own_heads * head
    owned = inner_weight.shape[0]
    length = rows * n_seq
    scale = head ** (-0.5)
    offset = -math.log(length)
    group = rows // 2
    hidden = expand_weight.shape[1] // 2
    share_hidden = hidden // n_seq
    slab = shrink_weight.shape[0]
    device = lax.axis_index(BOTH)
    sources = sources_of()

    inputs_low = tokens[0]
    upstream = cotangent[0]

    with jax.named_scope("inner"):
        gain_parts = share_small(norm_gains.astype(bf16).reshape(-1))
        small = jnp.concatenate([gain_parts.reshape(-1), document_index[0].astype(bf16)])
        small = jnp.pad(small[None], ((0, 15), (0, 3 * own_width - small.size)))
        inner_low = by_place(inner_weight.astype(bf16).reshape(owned, 3, n_seq, own_width), n_seq)
        small = jnp.broadcast_to(small, (n_seq, *small.shape))
        inner_blocks = exchange(jnp.concatenate([inner_low, small], axis=1))
        inner, inner_first = share_by_hand(inner_blocks[:, :owned].reshape(n_seq * owned, -1))
        small = inner_blocks[:, owned]
        gains = small[:, : gain_parts.size].reshape(n_seq, n_dp, 2, -1).astype(f32)
        gains = gains.transpose(2, 1, 0, 3).reshape(2, width)
        documents = small[:, gain_parts.size : gain_parts.size + rows]
        documents = jnp.concatenate([take(documents, s, 0) for s in sources]).astype(f32)
    with jax.named_scope("expand"):
        expand_low = expand_weight.astype(bf16).reshape(owned, 2 * n_dp, n_seq, slab)
        expand_low = by_place(expand_low, n_seq)
    with jax.named_scope("shrink"):
        shrink = share(shrink_weight.astype(bf16))
    gain_one, gain_two = gains[0], gains[1]

    groups = jnp.concatenate([lax.dynamic_slice_in_dim(group_order, 2 * s, 2) for s in sources])
    within = jnp.arange(group, dtype=jnp.int32)
    places = (groups[:, None] * group + within[None, :]).reshape(-1)
    cosine, sine = (part[:, 0] for part in angles(places, head))
    cosine, sine = jnp.concatenate([cosine] * 2, axis=1), jnp.concatenate([-sine, sine], axis=1)

    def turned(values, sign):
        half = head // 2
        swapped = jnp.concatenate([values[:, half:], values[:, :half]], axis=1)
        return values * cosine + swapped * (sine * sign)

    def head_of(array, part, h):
        start = (part * own_heads + h) * head
        return array[:, start : start + head]

    def first_norm(piece):
        values = piece.astype(f32)
        inverse = lax.rsqrt(jnp.mean(values * values, axis=-1, keepdims=True) + EPSILON)
        return values * inverse, inverse

    with jax.named_scope("tokens"):
        block = jnp.concatenate([inputs_low, outer_weight.astype(bf16)], axis=0)
        expand_sent = []

        def send_expand(last):
            expand_sent.append(after_in_place(expand_low, last))
            return expand_sent

        pieces, last = gather_rows(block, [inner_blocks, expand_low], [inner_first])
        expand_sent = [after_in_place(expand_low, last)]
        pieces = [piece.reshape(2, rows + owned, width) for piece in pieces]
        token_pieces = [piece[:, :rows].reshape(2 * rows, width) for piece in pieces]
    with jax.named_scope("outer"):
        outer = [piece[j, rows:] for piece in pieces for j in range(2)]
        outer[0] = after(outer[0], shrink)
        outer = share(in_place(outer).reshape(n_seq * owned, width))
    with jax.named_scope("expand"):
        expand_blocks = exchange(expand_sent[0])
    with jax.named_scope("attend"):
        attend_gain = after(gain_one, expand_sent[0])
        attend_pieces = [
            (first_norm(piece)[0] * attend_gain).astype(bf16) for piece in token_pieces
        ]
        projected = jnp.concatenate([multiply(piece, inner) for piece in attend_pieces], axis=0)
        visible = (documents[:, None] == documents[None, :]) & (places[None, :] <= places[:, None])
        visible = visible.astype(f32)
        query_rot, key_rot, value_low, weights, attended = [], [], [], [], []
        for h in range(own_heads):
            query_rot.append(turned(head_of(projected, 0, h), 1.0).astype(bf16))
            key_rot.append(turned(head_of(projected, 1, h), 1.0).astype(bf16))
            value_low.append(head_of(projected, 2, h).astype(bf16))
            scores = contract_last(query_rot[h], key_rot[h]) * scale + offset
            weights.append(jax.nn.sigmoid(scores) * visible)
            attended.append(multiply(weights[h].astype(bf16), value_low[h]).astype(bf16))
        attended = jnp.concatenate(attended, axis=1).reshape(n_seq, rows, own_width)

    with jax.named_scope("rows"):
        attended_rows = side_by_side(exchange_small(list(attended)))
    with jax.named_scope("expand"):
        expand_blocks = after_in_place(expand_blocks, attended_rows, outer)
        expand = share(expand_blocks.reshape(n_seq * owned, -1))
    inputs = inputs_low.astype(f32)
    residual = inputs + multiply(attended_rows, outer)
    inverse_second = lax.rsqrt(jnp.mean(residual * residual, axis=-1, keepdims=True) + EPSILON)
    normed_second = residual * inverse_second

    with jax.named_scope("mlp_input"):
        mlp_pieces, _ = gather_rows((normed_second * gain_two).astype(bf16))
    with jax.named_scope("gate_up"):
        gate_ups = [multiply(piece, expand) for piece in mlp_pieces]
    with jax.named_scope("cotangent"):
        upstream_pieces, _ = gather_rows(after(upstream, *mlp_pieces[1:]))
    activations, gate_up_grads = [None] * DEPTH, [None] * DEPTH

    def feed_back(k, earlier):
        gate, upward = gate_ups[k][:, :share_hidden], gate_ups[k][:, share_hidden:]
        gate = after(gate, *earlier)
        squash = jax.nn.sigmoid(gate)
        activations[k] = (gate * squash * upward).astype(bf16)
        down_grad = contract_last(upstream_pieces[k], shrink)
        d_gate = down_grad * upward * squash * (1.0 + gate * (1.0 - squash))
        d_upward = down_grad * gate * squash
        gate_up_grads[k] = jnp.concatenate([d_gate, d_upward], axis=1).astype(bf16)
        return contract_last(gate_up_grads[k], expand).astype(bf16)

    with jax.named_scope("d_mlp_input"):
        d_mlp_input, came = scatter_rows(feed_back, [0, 2, 1, 3])
    partial_gain_two = jnp.sum(d_mlp_input * normed_second, axis=0)
    d_residual = upstream.astype(f32) + norm_back(
        d_mlp_input * gain_two, normed_second, inverse_second
    )

    with jax.named_scope("heads"):
        d_residual_low = d_residual.astype(bf16)
        d_attended = contract_last(d_residual_low, outer).astype(bf16)
        d_attended = by_place(d_attended.reshape(rows, 1, n_seq, own_width), n_seq)
    with jax.named_scope("grad_expand"):
        grad_expand = contract_rows(
            jnp.concatenate(mlp_pieces, axis=0), jnp.concatenate(gate_up_grads, axis=0)
        )
        grad_expand = after(grad_expand, d_attended).astype(bf16)
    with jax.named_scope("heads"):
        d_attended = pick(exchange(d_attended), jnp.stack(sources)).reshape(length, own_width)
        d_attended = after(d_attended, grad_expand)
    with jax.named_scope("grad_expand"):
        grad_expand = reduce_over(grad_expand)
    with jax.named_scope("attend_back"):
        d_query, d_key, d_value = [], [], []
        for h in range(own_heads):
            d_out = head_of(d_attended, 0, h)
            d_weights = contract_last(d_out, value_low[h])
            d_scores = (d_weights * weights[h] * (1.0 - weights[h])).astype(bf16)
            d_query.append(turned(multiply(d_scores, key_rot[h]) * scale, -1.0))
            d_key.append(turned(contract_rows(d_scores, query_rot[h]) * scale, -1.0))
            d_value.append(contract_rows(weights[h].astype(bf16), d_out))
        d_projected = jnp.concatenate(
            [part.astype(bf16) for part in d_query + d_key + d_value], axis=1
        )
    with jax.named_scope("feed"):
        feed_terms = multiply(jnp.concatenate(activations, axis=0), shrink)
        feed_terms = after(feed_terms, d_residual_low).astype(bf16)
        feed_terms = feed_terms.reshape(DEPTH, 2, rows, width)
        feed = add_low(feed_terms[:, 0], across(feed_terms[:, 1]), d_projected)
        output = residual + feed[0].astype(f32)
        for k in range(1, DEPTH):
            output = output + turn(feed[k], k).astype(f32)
    with jax.named_scope("grad_shrink"):
        grad_shrink = contract_rows(
            jnp.concatenate(activations, axis=0), jnp.concatenate(upstream_pieces, axis=0)
        )
        grad_shrink = reduce_over(after(grad_shrink, d_projected).astype(bf16))
    with jax.named_scope("own_expand"):
        own_expand = exchange(grad_expand.reshape(n_seq, owned, -1))
    with jax.named_scope("grad_inner"):
        grad_inner = contract_rows(jnp.concatenate(attend_pieces, axis=0), d_projected)
        grad_inner_core = reduce_over_cores(grad_inner.astype(bf16))
        grad_inner = reduce_over_y(grad_inner_core)
    held = {FAR_FIRST[1]: [grad_inner_core], FAR_FIRST[2]: [feed], FAR_FIRST[3]: [own_expand]}
    gain_terms = [None] * DEPTH

    def attend_back(k, earlier):
        term = contract_last(d_projected[2 * rows * k : 2 * rows * (k + 1)], inner)
        term = after(term, *held.get(k, ()))
        gain_terms[k] = jnp.sum(term * first_norm(token_pieces[k])[0], axis=0)
        return term.astype(bf16)

    with jax.named_scope("d_attend_input"):
        d_attend_input, came_last = scatter_rows(attend_back, FAR_FIRST)
    d_attend_input = after(d_attend_input, output)
    partial_gain_one = sum(gain_terms)
    normed_first, inverse_first = first_norm(inputs_low)
    input_gradient = d_residual + norm_back(d_attend_input * gain_one, normed_first, inverse_first)

    with jax.named_scope("own_inner"):
        own_inner = exchange(grad_inner.reshape(n_seq, owned, -1))
    with jax.named_scope("grad_outer"):
        residual_grads, _ = gather_rows(d_residual_low)
        grad_outer = contract_rows(
            attended.reshape(length, own_width), jnp.concatenate(residual_grads, axis=0)
        )
        grad_outer = reduce_over_y(reduce_over_cores(grad_outer.astype(bf16)))
        grad_outer = move(
            grad_outer, lambda dp, z, x: (z, 2 * x + dp // 2, dp % 2)
        )

    local_squares = sum(
        jnp.sum(jnp.square(grad.astype(f32)))
        for grad in (grad_inner, grad_outer, grad_expand, grad_shrink)
    )
    with jax.named_scope("sums"):
        sums = jnp.concatenate(
            [partial_gain_one, partial_gain_two, jnp.full((128,), local_squares)]
        )
        sums = sum_everywhere(after(sums, d_attend_input).reshape(-1, 128)).reshape(-1)
    gains_whole = sums[: 2 * width].reshape(2, width)
    grad_gains = lax.dynamic_slice_in_dim(
        gains_whole, device * norm_gains.shape[1], norm_gains.shape[1], 1
    )
    global_norm = jnp.sqrt(sums[2 * width] + jnp.sum(gains_whole * gains_whole))
    factor = CLIP / jnp.maximum(global_norm, CLIP)

    results = [
        adamw_matrix(inner_weight, own_inner, first_inner, second_inner, factor, own_width),
        adamw_matrix(outer_weight, grad_outer, first_outer, second_outer, factor),
        adamw_matrix(expand_weight, own_expand, first_expand, second_expand, factor, slab),
        adamw_matrix(shrink_weight, grad_shrink, first_shrink, second_shrink, factor),
        adamw(norm_gains, grad_gains, first_gains, second_gains, factor, 0.0, GAIN_RATE),
    ]
    return (
        output[None],
        input_gradient[None],
        global_norm,
        *(result[0] for result in results),
        *(result[1] for result in results),
        *(result[2] for result in results),
    )


def project_in(normed, weight, gain):
    rows = normed.shape[0]

    def add_piece(carry, pieces, start):
        piece_left = (normed * pieces[1].astype(jnp.float32)).astype(jnp.bfloat16)
        partial_sum = jnp.dot(piece_left, pieces[0], preferred_element_type=jnp.float32)
        return (partial_sum, pieces[1])

    initial = (
        jnp.zeros((rows, weight.shape[1]), jnp.float32),
        jnp.zeros((normed.shape[1],), jnp.bfloat16),
    )
    product, full_gain = add_piece(
        initial,
        (
            lax.all_gather(weight.astype(jnp.bfloat16), ("dp", "seq"), axis=0, tiled=True),
            lax.all_gather(gain.astype(jnp.bfloat16), ("dp", "seq"), axis=0, tiled=True),
        ),
        jnp.int32(0),
    )
    left = (normed * full_gain.astype(jnp.float32)).astype(jnp.bfloat16)
    return (product, left, None, full_gain.astype(jnp.float32))


def project_mid(left, weight):

    def add_piece(partial_sum, piece, start):
        return jnp.dot(left, piece, preferred_element_type=jnp.float32)

    initial = jnp.zeros((left.shape[0], weight.shape[1]), jnp.float32)
    product = add_piece(
        initial,
        lax.all_gather(weight.astype(jnp.bfloat16), ("dp", "seq"), axis=0, tiled=True),
        jnp.int32(0),
    )
    return (product, None)


def weights_back(upstream, weight):
    return contract_last(
        upstream, lax.all_gather(weight.astype(jnp.bfloat16), ("dp", "seq"), axis=0, tiled=True)
    )


def reduce_in(left, upstream):
    owned = left.shape[1] // lax.axis_size(("dp", "seq"))

    def term(start, count):
        return contract_rows(left, upstream)

    return lax.psum_scatter(
        term(jnp.int32(0), lax.axis_size(("dp", "seq")) * owned),
        ("dp", "seq"),
        scatter_dimension=0,
        tiled=True,
    )


def reduce_mid(left, upstream):
    owned = left.shape[1] // lax.axis_size(("dp", "seq"))

    def term(start, count):
        return contract_rows(left, upstream)

    return lax.psum_scatter(
        term(jnp.int32(0), lax.axis_size(("dp", "seq")) * owned),
        ("dp", "seq"),
        scatter_dimension=0,
        tiled=True,
    )


def gathered_body(
    tokens,
    cotangent,
    inner_weight,
    outer_weight,
    expand_weight,
    shrink_weight,
    norm_gains,
    first_inner,
    first_outer,
    first_expand,
    first_shrink,
    first_gains,
    second_inner,
    second_outer,
    second_expand,
    second_shrink,
    second_gains,
    document_index,
    group_order,
):
    inputs = tokens[0].astype(jnp.float32)
    rows, width = inputs.shape
    head_size = width // HEADS
    length = rows * lax.axis_size("seq")
    scale = head_size ** (-0.5)
    offset = -math.log(length)
    group = rows // 2
    within = jnp.arange(group, dtype=jnp.int32)
    paired = lax.dynamic_slice_in_dim(group_order, 2 * lax.axis_index("seq"), 2)
    own_place = (paired[:, None] * group + within[None, :]).reshape(-1)
    all_places = (group_order[:, None] * group + within[None, :]).reshape(-1)
    own_document = document_index[0].astype(jnp.bfloat16)
    cosine, sine = angles(own_place, head_size)
    inverse_first = lax.rsqrt(jnp.mean(inputs * inputs, axis=-1, keepdims=True) + EPSILON)
    normed_first = inputs * inverse_first
    projected, attend_input, kept_inner, gain_one = project_in(
        normed_first, inner_weight, norm_gains[0]
    )
    queries = projected[:, :width].reshape(rows, HEADS, head_size)
    query_rot = rotate(queries, cosine, sine).astype(jnp.bfloat16)
    key_rot = rotate(projected[:, width : 2 * width].reshape(rows, HEADS, head_size), cosine, sine)
    key_rot = key_rot.reshape(rows, width).astype(jnp.bfloat16)
    value_low = projected[:, 2 * width :].astype(jnp.bfloat16)

    def sigmoid_weights(key_piece, document_piece):
        count = key_piece.shape[0]
        scores = (
            jnp.einsum(
                "qhd,khd->hqk",
                query_rot,
                key_piece.reshape(count, HEADS, head_size),
                preferred_element_type=jnp.float32,
            )
            * scale
            + offset
        )
        visible = (own_document[:, None] == document_piece[None, :]) & (
            all_places[None, :] <= own_place[:, None]
        )
        return jax.nn.sigmoid(scores) * visible.astype(jnp.float32)[None]

    key_piece = lax.all_gather(key_rot, "seq", axis=0, tiled=True)
    value_piece = lax.all_gather(value_low, "seq", axis=0, tiled=True)
    document_piece = lax.all_gather(own_document, "seq", axis=0, tiled=True)
    count = key_piece.shape[0]
    weights = sigmoid_weights(key_piece, document_piece).astype(jnp.bfloat16)
    attended = jnp.einsum(
        "hqk,khd->qhd",
        weights,
        value_piece.reshape(count, HEADS, head_size),
        preferred_element_type=jnp.float32,
    )
    attended = attended.reshape(rows, width).astype(jnp.bfloat16)
    branch, kept_outer = project_mid(attended, outer_weight)
    residual = inputs + branch
    inverse_second = lax.rsqrt(jnp.mean(residual * residual, axis=-1, keepdims=True) + EPSILON)
    normed_second = residual * inverse_second
    gate_up, mlp_input, kept_expand, gain_two = project_in(
        normed_second, expand_weight, norm_gains[1]
    )
    hidden = gate_up.shape[1] // 2
    gate = gate_up[:, :hidden]
    upward = gate_up[:, hidden:]
    squash = jax.nn.sigmoid(gate)
    activation = (gate * squash * upward).astype(jnp.bfloat16)
    feed, kept_shrink = project_mid(activation, shrink_weight)
    output = residual + feed
    upstream = cotangent[0]
    down_grad = weights_back(upstream, shrink_weight)
    grad_shrink = reduce_mid(activation, upstream)
    d_gate = down_grad * upward * squash * (1.0 + gate * (1.0 - squash))
    d_upward = down_grad * gate * squash
    d_gate_up = jnp.concatenate([d_gate, d_upward], axis=1).astype(jnp.bfloat16)
    d_mlp_input = weights_back(d_gate_up, expand_weight)
    grad_expand = reduce_in(mlp_input, d_gate_up)
    partial_gain_two = jnp.sum(d_mlp_input * normed_second, axis=0)
    d_residual = upstream.astype(jnp.float32) + norm_back(
        d_mlp_input * gain_two, normed_second, inverse_second
    )
    d_residual_low = d_residual.astype(jnp.bfloat16)
    d_attended = weights_back(d_residual_low, outer_weight)
    grad_outer = reduce_mid(attended, d_residual_low)
    d_attended_flat = d_attended.astype(jnp.bfloat16)
    d_attended_low = d_attended_flat.reshape(rows, HEADS, head_size)
    key_piece = lax.all_gather(key_rot, "seq", axis=0, tiled=True)
    value_piece = lax.all_gather(value_low, "seq", axis=0, tiled=True)
    document_piece = lax.all_gather(own_document, "seq", axis=0, tiled=True)
    count = key_piece.shape[0]
    score_count = key_piece.shape[0]
    weights = sigmoid_weights(key_piece, document_piece)
    d_weights = jnp.einsum(
        "qhd,khd->hqk",
        d_attended_low,
        value_piece.reshape(score_count, HEADS, head_size),
        preferred_element_type=jnp.float32,
    )
    d_scores = (d_weights * weights * (1.0 - weights)).astype(jnp.bfloat16)
    weights, d_scores, key_heads = (
        weights,
        d_scores,
        key_piece.reshape(score_count, HEADS, head_size),
    )
    d_query = (
        jnp.einsum("hqk,khd->qhd", d_scores, key_heads, preferred_element_type=jnp.float32) * scale
    )
    key_term = (
        jnp.einsum("hqk,qhd->khd", d_scores, query_rot, preferred_element_type=jnp.float32) * scale
    )
    value_term = jnp.einsum(
        "hqk,qhd->khd",
        weights.astype(jnp.bfloat16),
        d_attended_low,
        preferred_element_type=jnp.float32,
    )
    d_keys = key_term.reshape(count, width)
    d_values = value_term.reshape(count, width)
    backward_sums = (d_query, d_keys, d_values)
    d_query = backward_sums[0]
    key_grad, value_grad = (
        lax.psum_scatter(
            backward_sums[1].astype(jnp.bfloat16), "seq", scatter_dimension=0, tiled=True
        ).astype(jnp.float32),
        lax.psum_scatter(
            backward_sums[2].astype(jnp.bfloat16), "seq", scatter_dimension=0, tiled=True
        ).astype(jnp.float32),
    )
    d_projected = jnp.concatenate(
        [
            unrotate(d_query, cosine, sine).reshape(rows, width),
            unrotate(key_grad.reshape(rows, HEADS, head_size), cosine, sine).reshape(rows, width),
            value_grad,
        ],
        axis=1,
    ).astype(jnp.bfloat16)
    d_attend_input = weights_back(d_projected, inner_weight)
    grad_inner = reduce_in(attend_input, d_projected)
    partial_gain_one = jnp.sum(d_attend_input * normed_first, axis=0)
    input_gradient = d_residual + norm_back(d_attend_input * gain_one, normed_first, inverse_first)
    local_squares = (
        jnp.sum(grad_inner * grad_inner)
        + jnp.sum(grad_outer * grad_outer)
        + jnp.sum(grad_expand * grad_expand)
    )
    local_squares = local_squares + jnp.sum(grad_shrink * grad_shrink)
    matrix_squares, gains_whole = lax.psum(
        (local_squares, jnp.stack([partial_gain_one, partial_gain_two])), ("dp", "seq")
    )
    owned_gains = norm_gains.shape[1]
    grad_gains = lax.dynamic_slice_in_dim(
        gains_whole, lax.axis_index(("dp", "seq")) * owned_gains, owned_gains, 1
    )
    global_norm = jnp.sqrt(matrix_squares + jnp.sum(gains_whole * gains_whole))
    factor = CLIP / jnp.maximum(global_norm, CLIP)
    gradients = (grad_inner, grad_outer, grad_expand, grad_shrink, grad_gains)
    masters = (inner_weight, outer_weight, expand_weight, shrink_weight, norm_gains)
    firsts = (first_inner, first_outer, first_expand, first_shrink, first_gains)
    seconds = (second_inner, second_outer, second_expand, second_shrink, second_gains)
    decays = (DECAY, DECAY, DECAY, DECAY, 0.0)
    rates = (RATE, RATE, RATE, RATE, GAIN_RATE)
    results = [
        adamw(
            masters[index],
            gradients[index],
            firsts[index],
            seconds[index],
            factor,
            decays[index],
            rates[index],
        )
        for index in range(5)
    ]
    return (
        output[None],
        input_gradient[None],
        global_norm,
        results[0][0],
        results[1][0],
        results[2][0],
        results[3][0],
        results[4][0],
        results[0][1],
        results[1][1],
        results[2][1],
        results[3][1],
        results[4][1],
        results[0][2],
        results[1][2],
        results[2][2],
        results[3][2],
        results[4][2],
    )


def solution(mesh):
    whole_heads = mesh.shape["seq"] == 2 * DEPTH and mesh.shape["dp"] == 4
    placed = (
        P("dp", "seq", None),
        P("dp", "seq", None),
        P(("dp", "seq"), None),
        P(("dp", "seq"), None),
        P(("dp", "seq"), None),
        P(("dp", "seq"), None),
        P(None, ("dp", "seq")),
        P(("dp", "seq"), None),
        P(("dp", "seq"), None),
        P(("dp", "seq"), None),
        P(("dp", "seq"), None),
        P(None, ("dp", "seq")),
        P(("dp", "seq"), None),
        P(("dp", "seq"), None),
        P(("dp", "seq"), None),
        P(("dp", "seq"), None),
        P(None, ("dp", "seq")),
        P("dp", "seq"),
        P(),
    )
    return jax.shard_map(
        body if whole_heads else gathered_body,
        mesh=mesh,
        in_specs=placed,
        out_specs=(
            P("dp", "seq", None),
            P("dp", "seq", None),
            P(),
            P(("dp", "seq"), None),
            P(("dp", "seq"), None),
            P(("dp", "seq"), None),
            P(("dp", "seq"), None),
            P(None, ("dp", "seq")),
            P(("dp", "seq"), None),
            P(("dp", "seq"), None),
            P(("dp", "seq"), None),
            P(("dp", "seq"), None),
            P(None, ("dp", "seq")),
            P(("dp", "seq"), None),
            P(("dp", "seq"), None),
            P(("dp", "seq"), None),
            P(("dp", "seq"), None),
            P(None, ("dp", "seq")),
        ),
        check_vma=False,
    )
```

```python
import math

import jax
import jax.numpy as jnp
from jax import lax
from jax.experimental import pallas as pl
from jax.experimental.pallas import tpu as pltpu
from jax.sharding import PartitionSpec as P

HEADS = 16
STEP = 10


EPSILON = 1e-05
THETA = 10000.0
BETA_ONE = 0.9
BETA_TWO = 0.95
RATE = 0.05
GAIN_RATE = 0.5
DECAY = 0.1
ADAM_EPSILON = 1e-08
CLIP = 1.0
BOTH = ("dp", "seq")


def angles(positions, width):
    frequency = THETA ** (-(jnp.arange(width // 2, dtype=jnp.float32) * 2.0) / width)
    turned = positions.astype(jnp.float32)[:, None] * frequency[None, :]
    return (jnp.cos(turned)[:, None, :], jnp.sin(turned)[:, None, :])


def rotate(values, cosine, sine):
    half = values.shape[-1] // 2
    first, second = (values[..., :half], values[..., half:])
    return jnp.concatenate(
        [first * cosine - second * sine, second * cosine + first * sine], axis=-1
    )


def unrotate(upstream, cosine, sine):
    half = upstream.shape[-1] // 2
    first, second = (upstream[..., :half], upstream[..., half:])
    return jnp.concatenate(
        [first * cosine + second * sine, second * cosine - first * sine], axis=-1
    )


def norm_back(upstream, normed, inverse):
    return inverse * (upstream - normed * jnp.mean(upstream * normed, axis=-1, keepdims=True))


def contract_rows(left, right):
    return lax.dot_general(
        left, right, (((0,), (0,)), ((), ())), preferred_element_type=jnp.float32
    )


def contract_last(left, right):
    return lax.dot_general(
        left, right, (((1,), (1,)), ((), ())), preferred_element_type=jnp.float32
    )


def multiply(left, right):
    return jnp.dot(left, right, preferred_element_type=jnp.float32)


def adamw(weight, grad, first, second, factor, decay, rate):
    grad = grad * factor
    first = BETA_ONE * first + (1.0 - BETA_ONE) * grad
    second = BETA_TWO * second + (1.0 - BETA_TWO) * grad * grad
    update = (
        first / (1.0 - BETA_ONE**STEP) / (jnp.sqrt(second / (1.0 - BETA_TWO**STEP)) + ADAM_EPSILON)
    )
    return (first, second, weight - rate * (update + decay * weight))


def adamw_blocks(factor, weight, grad, first, second, weight_new, first_new, second_new):
    count = grad.shape[0] if len(grad.shape) == 3 else 1
    size = weight.shape[1] // count
    for index in range(count):
        columns = pl.ds(index * size, size)
        low = grad[index] if len(grad.shape) == 3 else grad[...]
        result = adamw(
            weight[:, columns],
            low.astype(jnp.float32),
            first[:, columns],
            second[:, columns],
            factor[0],
            DECAY,
            RATE,
        )
        first_new[:, columns], second_new[:, columns], weight_new[:, columns] = result


def adamw_matrix(weight, grad, first, second, factor, size=0):
    rows, columns = weight.shape
    if grad.ndim == 3:
        places = grad.shape[0]
        grad_spec = pl.BlockSpec((places, rows, size), lambda i: (0, 0, i))
        grid = (grad.shape[2] // size,)
        spec = pl.BlockSpec((rows, places * size), lambda i: (0, i))
    else:
        grid = (rows // 64,)
        spec = grad_spec = pl.BlockSpec((64, columns), lambda i: (i, 0))
    result = jax.ShapeDtypeStruct(weight.shape, jnp.float32)
    weight_new, first_new, second_new = pl.pallas_call(
        adamw_blocks,
        grid=grid,
        in_specs=[pl.BlockSpec(memory_space=pltpu.SMEM), spec, grad_spec, spec, spec],
        out_specs=[spec, spec, spec],
        out_shape=[result, result, result],
        compiler_params=pltpu.CompilerParams(vmem_limit_bytes=56 * 1024 * 1024),
        cost_estimate=pl.CostEstimate(
            flops=20 * weight.size, bytes_accessed=26 * weight.size, transcendentals=weight.size
        ),
    )(factor.reshape(1), weight, grad, first, second)
    return first_new, second_new, weight_new


def move(value, where):
    pairs = []
    for dp in range(lax.axis_size("dp")):
        for seq in range(lax.axis_size("seq")):
            target = where(dp, seq // 2, seq % 2)
            if target is not None:
                pairs.append(
                    (
                        dp * lax.axis_size("seq") + seq,
                        target[0] * lax.axis_size("seq") + target[1] * 2 + target[2],
                    )
                )
    return lax.ppermute(value, BOTH, pairs)


FAR_FIRST = [2, 3, 1, 0]
DEPTH = 4


def across(value):
    return move(value, lambda dp, z, x: (dp, z, 1 - x))


def turn(value, k):
    return move(value, lambda dp, z, x: (dp, z ^ k, x))


def line(value, hop, direction):
    def where(dp, z, x):
        if direction > 0:
            return (dp, z + 1, x) if z >= hop - 1 and z + 1 < DEPTH else None
        return (dp, z - 1, x) if z <= DEPTH - hop and z >= 1 else None

    return move(value, where)


def gather_rows(block, first_holds=(), last_holds=(), crossing=None):
    z = lax.axis_index("seq") // 2
    column, other = [block], [across(block)]

    def came(piece, *holds):
        column.append(after(piece, other[-1], *holds))
        other.append(across(column[-1]))

    up, down = line(block, 1, 1), line(block, 1, -1)
    up_one, down_one = up, down
    came(jnp.where(z % 2 == 0, down, up))
    up, down = line(after(up, *first_holds), 2, 1), line(after(down, *first_holds), 2, -1)
    came(jnp.where(z < 2, down, up))
    last_holds = (other[1], *last_holds)
    up, down = line(after(up, *last_holds), 3, 1), line(after(down, *last_holds), 3, -1)
    last = jnp.where(z < 2, jnp.where(z == 0, down, down_one), jnp.where(z == 3, up, up_one))
    came(last, *(crossing(last) if crossing else ()))
    return [jnp.concatenate(pair, axis=0) for pair in zip(column, other, strict=True)], column[-1]


def nothing(*others):
    firsts = [lax.slice(other, (0,) * other.ndim, (1,) * other.ndim) for other in others]
    return sum(first.reshape(()).astype(jnp.float32) for first in firsts) * 0.0


def after(value, *others):
    return value + nothing(*others).astype(value.dtype) if others else value


def after_in_place(value, *others):
    value = lax.optimization_barrier(value)
    start = (0,) * value.ndim
    first = lax.slice(value, start, (1,) * (value.ndim - 1) + (128,))
    return lax.dynamic_update_slice(value, after(first, *others), start)


def pairs_of():
    return [(k, j) for k in range(DEPTH) for j in range(2)]


def sources_of():
    z, x = lax.axis_index("seq") // 2, lax.axis_index("seq") % 2
    return [(z ^ k) * 2 + (x ^ j) for k, j in pairs_of()]


def exchange(blocks):
    return lax.all_to_all(blocks, "seq", 0, 0, tiled=True)


def exchange_small(blocks):
    return [
        move(block, lambda dp, z, x: (dp, z ^ k, x ^ j)) if (k, j) != (0, 0) else block
        for (k, j), block in zip(pairs_of(), blocks, strict=True)
    ]


def by_place(columns, n_seq):
    rows, groups, _, size = columns.shape
    return columns.transpose(2, 0, 1, 3).reshape(n_seq, rows, -1)


def copy_block(order, source, target):
    target[...] = source[...]


def pick(blocks, order):
    count, rows, columns = blocks.shape
    block = (1, rows, columns)
    return pl.pallas_call(
        copy_block,
        grid_spec=pltpu.PrefetchScalarGridSpec(
            num_scalar_prefetch=1,
            grid=(count,),
            in_specs=[pl.BlockSpec(block, lambda i, order: (order[i], 0, 0))],
            out_specs=pl.BlockSpec(block, lambda i, order: (i, 0, 0)),
        ),
        out_shape=jax.ShapeDtypeStruct(blocks.shape, blocks.dtype),
        compiler_params=pltpu.CompilerParams(vmem_limit_bytes=56 * 1024 * 1024),
        cost_estimate=pl.CostEstimate(flops=0, bytes_accessed=4 * blocks.size, transcendentals=0),
    )(order.astype(jnp.int32), blocks)


def in_place(received):
    return pick(jnp.stack(received), jnp.stack(sources_of()))


def side_by_side(received):
    count, (rows, columns) = len(received), received[0].shape
    return pl.pallas_call(
        copy_block,
        grid_spec=pltpu.PrefetchScalarGridSpec(
            num_scalar_prefetch=1,
            grid=(count,),
            in_specs=[pl.BlockSpec((None, rows, columns), lambda i, order: (order[i], 0, 0))],
            out_specs=pl.BlockSpec((rows, columns), lambda i, order: (0, i)),
        ),
        out_shape=jax.ShapeDtypeStruct((rows, count * columns), received[0].dtype),
        compiler_params=pltpu.CompilerParams(vmem_limit_bytes=56 * 1024 * 1024),
        cost_estimate=pl.CostEstimate(
            flops=0, bytes_accessed=4 * count * rows * columns, transcendentals=0
        ),
    )(jnp.stack(sources_of()).astype(jnp.int32), jnp.stack(received))


def scatter_rows(partial, order):
    sums, came = {}, []
    for n, k in enumerate(order):
        earlier = came[n - 2 : n - 1] if n >= 2 else []
        if n == DEPTH - 1:
            earlier = earlier + [sums[order[0]]] if order[0] else earlier
        term = partial(k, earlier)
        rows = term.shape[0] // 2
        came.append(across(term[rows:]))
        total = term[:rows].astype(jnp.float32) + came[-1].astype(jnp.float32)
        sums[k] = turn(total.astype(jnp.bfloat16), k) if k else total
    return sum(sums[k].astype(jnp.float32) for k in range(DEPTH)), came


def sum_everywhere(value):
    def of_four(where):
        others = [move(value, lambda dp, z, x: where(dp, z, x, mask)) for mask in (1, 2, 3)]
        return (value + others[0]) + (others[1] + others[2])

    value = of_four(lambda dp, z, x, mask: (dp ^ mask, z, x))
    value = of_four(lambda dp, z, x, mask: (dp, z ^ mask, x))
    return value + across(value)


def other_core(value):
    return move(value, lambda dp, z, x: (dp ^ 1, z, x))


def other_y(value):
    return move(value, lambda dp, z, x: (dp ^ 2, z, x))


def share(rows):
    return lax.all_gather(rows, "dp", axis=0, tiled=True)


def share_by_hand(rows):
    dp = lax.axis_index("dp")
    pair = jnp.stack([rows, other_y(rows)])
    other = other_core(pair)
    masks = [at ^ dp for at in range(4)]
    order = jnp.stack([(mask % 2) * 2 + mask // 2 for mask in masks])
    whole = pick(jnp.concatenate([pair, other]), order)
    return whole.reshape(-1, *rows.shape[1:]), pair[1]


def share_small(value):
    dp = lax.axis_index("dp")
    whole = jnp.zeros((4, *value.shape), value.dtype)
    for mask in range(4):
        piece = move(value, lambda dp, z, x: (dp ^ mask, z, x)) if mask else value
        whole = lax.dynamic_update_index_in_dim(whole, piece, dp ^ mask, 0)
    return whole


def reduce_over(rows):
    return lax.psum_scatter(rows, "dp", scatter_dimension=0, tiled=True)


def take(array, index, axis):
    return lax.dynamic_index_in_dim(array, index, axis, keepdims=False)


def add_low(left, right, *holds):
    total = left.astype(jnp.float32) + right.astype(jnp.float32)
    return after(total, *holds).astype(jnp.bfloat16)


def reduce_over_cores(rows):
    core = lax.axis_index("dp") % 2
    parts = rows.reshape(2, 2, -1, *rows.shape[1:])
    return add_low(take(parts, core, 1), other_core(take(parts, 1 - core, 1)))


def reduce_over_y(parts):
    y = lax.axis_index("dp") // 2
    return add_low(take(parts, y, 0), other_y(take(parts, 1 - y, 0)))


def body(
    tokens,
    cotangent,
    inner_weight,
    outer_weight,
    expand_weight,
    shrink_weight,
    norm_gains,
    first_inner,
    first_outer,
    first_expand,
    first_shrink,
    first_gains,
    second_inner,
    second_outer,
    second_expand,
    second_shrink,
    second_gains,
    document_index,
    group_order,
):
    bf16, f32 = jnp.bfloat16, jnp.float32
    rows, width = tokens.shape[1:]
    n_dp, n_seq = lax.axis_size("dp"), lax.axis_size("seq")
    head = width // HEADS
    own_heads = HEADS // n_seq
    own_width = own_heads * head
    owned = inner_weight.shape[0]
    length = rows * n_seq
    scale = head ** (-0.5)
    offset = -math.log(length)
    group = rows // 2
    hidden = expand_weight.shape[1] // 2
    share_hidden = hidden // n_seq
    slab = shrink_weight.shape[0]
    device = lax.axis_index(BOTH)
    sources = sources_of()

    inputs_low = tokens[0]
    upstream = cotangent[0]

    with jax.named_scope("inner"):
        gain_parts = share_small(norm_gains.astype(bf16).reshape(-1))
        small = jnp.concatenate([gain_parts.reshape(-1), document_index[0].astype(bf16)])
        small = jnp.pad(small[None], ((0, 15), (0, 3 * own_width - small.size)))
        inner_low = by_place(inner_weight.astype(bf16).reshape(owned, 3, n_seq, own_width), n_seq)
        small = jnp.broadcast_to(small, (n_seq, *small.shape))
        inner_blocks = exchange(jnp.concatenate([inner_low, small], axis=1))
        inner, inner_first = share_by_hand(inner_blocks[:, :owned].reshape(n_seq * owned, -1))
        small = inner_blocks[:, owned]
        gains = small[:, : gain_parts.size].reshape(n_seq, n_dp, 2, -1).astype(f32)
        gains = gains.transpose(2, 1, 0, 3).reshape(2, width)
        documents = small[:, gain_parts.size : gain_parts.size + rows]
        documents = jnp.concatenate([take(documents, s, 0) for s in sources]).astype(f32)
    with jax.named_scope("expand"):
        expand_low = expand_weight.astype(bf16).reshape(owned, 2 * n_dp, n_seq, slab)
        expand_low = by_place(expand_low, n_seq)
    with jax.named_scope("shrink"):
        shrink = share(shrink_weight.astype(bf16))
    gain_one, gain_two = gains[0], gains[1]

    groups = jnp.concatenate([lax.dynamic_slice_in_dim(group_order, 2 * s, 2) for s in sources])
    within = jnp.arange(group, dtype=jnp.int32)
    places = (groups[:, None] * group + within[None, :]).reshape(-1)
    cosine, sine = (part[:, 0] for part in angles(places, head))
    cosine, sine = jnp.concatenate([cosine] * 2, axis=1), jnp.concatenate([-sine, sine], axis=1)

    def turned(values, sign):
        half = head // 2
        swapped = jnp.concatenate([values[:, half:], values[:, :half]], axis=1)
        return values * cosine + swapped * (sine * sign)

    def head_of(array, part, h):
        start = (part * own_heads + h) * head
        return array[:, start : start + head]

    def first_norm(piece):
        values = piece.astype(f32)
        inverse = lax.rsqrt(jnp.mean(values * values, axis=-1, keepdims=True) + EPSILON)
        return values * inverse, inverse

    with jax.named_scope("tokens"):
        block = jnp.concatenate([inputs_low, outer_weight.astype(bf16)], axis=0)
        expand_sent = []

        def send_expand(last):
            expand_sent.append(after_in_place(expand_low, last))
            return expand_sent

        pieces, last = gather_rows(block, [inner_blocks, expand_low], [inner_first])
        expand_sent = [after_in_place(expand_low, last)]
        pieces = [piece.reshape(2, rows + owned, width) for piece in pieces]
        token_pieces = [piece[:, :rows].reshape(2 * rows, width) for piece in pieces]
    with jax.named_scope("outer"):
        outer = [piece[j, rows:] for piece in pieces for j in range(2)]
        outer[0] = after(outer[0], shrink)
        outer = share(in_place(outer).reshape(n_seq * owned, width))
    with jax.named_scope("expand"):
        expand_blocks = exchange(expand_sent[0])
    with jax.named_scope("attend"):
        attend_gain = after(gain_one, expand_sent[0])
        attend_pieces = [
            (first_norm(piece)[0] * attend_gain).astype(bf16) for piece in token_pieces
        ]
        projected = jnp.concatenate([multiply(piece, inner) for piece in attend_pieces], axis=0)
        visible = (documents[:, None] == documents[None, :]) & (places[None, :] <= places[:, None])
        visible = visible.astype(f32)
        query_rot, key_rot, value_low, weights, attended = [], [], [], [], []
        for h in range(own_heads):
            query_rot.append(turned(head_of(projected, 0, h), 1.0).astype(bf16))
            key_rot.append(turned(head_of(projected, 1, h), 1.0).astype(bf16))
            value_low.append(head_of(projected, 2, h).astype(bf16))
            scores = contract_last(query_rot[h], key_rot[h]) * scale + offset
            weights.append(jax.nn.sigmoid(scores) * visible)
            attended.append(multiply(weights[h].astype(bf16), value_low[h]).astype(bf16))
        attended = jnp.concatenate(attended, axis=1).reshape(n_seq, rows, own_width)

    with jax.named_scope("rows"):
        attended_rows = side_by_side(exchange_small(list(attended)))
    with jax.named_scope("expand"):
        expand_blocks = after_in_place(expand_blocks, attended_rows, outer)
        expand = share(expand_blocks.reshape(n_seq * owned, -1))
    inputs = inputs_low.astype(f32)
    residual = inputs + multiply(attended_rows, outer)
    inverse_second = lax.rsqrt(jnp.mean(residual * residual, axis=-1, keepdims=True) + EPSILON)
    normed_second = residual * inverse_second

    with jax.named_scope("mlp_input"):
        mlp_pieces, _ = gather_rows((normed_second * gain_two).astype(bf16))
    with jax.named_scope("gate_up"):
        gate_ups = [multiply(piece, expand) for piece in mlp_pieces]
    with jax.named_scope("cotangent"):
        upstream_pieces, _ = gather_rows(after(upstream, *mlp_pieces[1:]), (), gate_ups[:1])
    activations, gate_up_grads = [None] * DEPTH, [None] * DEPTH

    def feed_back(k, earlier):
        gate, upward = gate_ups[k][:, :share_hidden], gate_ups[k][:, share_hidden:]
        gate = after(gate, *earlier)
        squash = jax.nn.sigmoid(gate)
        activations[k] = (gate * squash * upward).astype(bf16)
        down_grad = contract_last(upstream_pieces[k], shrink)
        d_gate = down_grad * upward * squash * (1.0 + gate * (1.0 - squash))
        d_upward = down_grad * gate * squash
        gate_up_grads[k] = jnp.concatenate([d_gate, d_upward], axis=1).astype(bf16)
        return contract_last(gate_up_grads[k], expand).astype(bf16)

    with jax.named_scope("d_mlp_input"):
        d_mlp_input, came = scatter_rows(feed_back, [0, 2, 1, 3])
    partial_gain_two = jnp.sum(d_mlp_input * normed_second, axis=0)
    d_residual = upstream.astype(f32) + norm_back(
        d_mlp_input * gain_two, normed_second, inverse_second
    )

    with jax.named_scope("heads"):
        d_residual_low = d_residual.astype(bf16)
        d_attended = contract_last(d_residual_low, outer).astype(bf16)
        d_attended = by_place(d_attended.reshape(rows, 1, n_seq, own_width), n_seq)
    with jax.named_scope("grad_expand"):
        grad_expand = contract_rows(
            jnp.concatenate(mlp_pieces, axis=0), jnp.concatenate(gate_up_grads, axis=0)
        )
        grad_expand = after(grad_expand, d_attended).astype(bf16)
    with jax.named_scope("heads"):
        d_attended = pick(exchange(d_attended), jnp.stack(sources)).reshape(length, own_width)
        d_attended = after(d_attended, grad_expand)
    with jax.named_scope("grad_expand"):
        grad_expand = reduce_over(grad_expand)
    with jax.named_scope("attend_back"):
        d_query, d_key, d_value = [], [], []
        for h in range(own_heads):
            d_out = head_of(d_attended, 0, h)
            d_weights = contract_last(d_out, value_low[h])
            d_scores = (d_weights * weights[h] * (1.0 - weights[h])).astype(bf16)
            d_query.append(turned(multiply(d_scores, key_rot[h]) * scale, -1.0))
            d_key.append(turned(contract_rows(d_scores, query_rot[h]) * scale, -1.0))
            d_value.append(contract_rows(weights[h].astype(bf16), d_out))
        d_projected = jnp.concatenate(
            [part.astype(bf16) for part in d_query + d_key + d_value], axis=1
        )
    with jax.named_scope("feed"):
        feed_terms = multiply(jnp.concatenate(activations, axis=0), shrink)
        feed_terms = after(feed_terms, d_residual_low).astype(bf16)
        feed_terms = feed_terms.reshape(DEPTH, 2, rows, width)
        feed = add_low(feed_terms[:, 0], across(feed_terms[:, 1]), d_projected)
        output = residual + feed[0].astype(f32)
        for k in range(1, DEPTH):
            output = output + turn(feed[k], k).astype(f32)
    with jax.named_scope("grad_shrink"):
        grad_shrink = contract_rows(
            jnp.concatenate(activations, axis=0), jnp.concatenate(upstream_pieces, axis=0)
        )
        grad_shrink = reduce_over(after(grad_shrink, d_projected).astype(bf16))
    with jax.named_scope("own_expand"):
        own_expand = exchange(grad_expand.reshape(n_seq, owned, -1))
    with jax.named_scope("grad_inner"):
        grad_inner = contract_rows(jnp.concatenate(attend_pieces, axis=0), d_projected)
        grad_inner_core = reduce_over_cores(grad_inner.astype(bf16))
        grad_inner = reduce_over_y(grad_inner_core)
    held = {FAR_FIRST[1]: [grad_inner_core], FAR_FIRST[2]: [feed], FAR_FIRST[3]: [own_expand]}
    gain_terms = [None] * DEPTH

    def attend_back(k, earlier):
        term = contract_last(d_projected[2 * rows * k : 2 * rows * (k + 1)], inner)
        term = after(term, *held.get(k, ()))
        gain_terms[k] = jnp.sum(term * first_norm(token_pieces[k])[0], axis=0)
        return term.astype(bf16)

    with jax.named_scope("d_attend_input"):
        d_attend_input, came_last = scatter_rows(attend_back, FAR_FIRST)
    d_attend_input = after(d_attend_input, output)
    partial_gain_one = sum(gain_terms)
    normed_first, inverse_first = first_norm(inputs_low)
    input_gradient = d_residual + norm_back(d_attend_input * gain_one, normed_first, inverse_first)

    with jax.named_scope("grad_outer"):
        residual_grads, _ = gather_rows(d_residual_low)
        grad_outer = contract_rows(
            attended.reshape(length, own_width), jnp.concatenate(residual_grads, axis=0)
        )
        grad_outer = reduce_over_y(reduce_over_cores(grad_outer.astype(bf16)))
        grad_outer = move(
            grad_outer, lambda dp, z, x: (z, 2 * x + dp // 2, dp % 2)
        )

    local_squares = sum(
        jnp.sum(jnp.square(grad.astype(f32)))
        for grad in (grad_inner, grad_outer, grad_expand, grad_shrink)
    )
    with jax.named_scope("sums"):
        sums = jnp.concatenate(
            [partial_gain_one, partial_gain_two, jnp.full((128,), local_squares)]
        )
        sums = sum_everywhere(after(sums, d_attend_input).reshape(-1, 128)).reshape(-1)
    gains_whole = sums[: 2 * width].reshape(2, width)
    grad_gains = lax.dynamic_slice_in_dim(
        gains_whole, device * norm_gains.shape[1], norm_gains.shape[1], 1
    )
    global_norm = jnp.sqrt(sums[2 * width] + jnp.sum(gains_whole * gains_whole))
    factor = CLIP / jnp.maximum(global_norm, CLIP)

    with jax.named_scope("own_inner"):
        own_inner = after_in_place(grad_inner, factor)
        own_inner = exchange(own_inner.reshape(n_seq, owned, -1))
    results = [
        adamw_matrix(inner_weight, own_inner, first_inner, second_inner, factor, own_width),
        adamw_matrix(outer_weight, grad_outer, first_outer, second_outer, factor),
        adamw_matrix(expand_weight, own_expand, first_expand, second_expand, factor, slab),
        adamw_matrix(shrink_weight, grad_shrink, first_shrink, second_shrink, factor),
        adamw(norm_gains, grad_gains, first_gains, second_gains, factor, 0.0, GAIN_RATE),
    ]
    return (
        output[None],
        input_gradient[None],
        global_norm,
        *(result[0] for result in results),
        *(result[1] for result in results),
        *(result[2] for result in results),
    )


def project_in(normed, weight, gain):
    rows = normed.shape[0]

    def add_piece(carry, pieces, start):
        piece_left = (normed * pieces[1].astype(jnp.float32)).astype(jnp.bfloat16)
        partial_sum = jnp.dot(piece_left, pieces[0], preferred_element_type=jnp.float32)
        return (partial_sum, pieces[1])

    initial = (
        jnp.zeros((rows, weight.shape[1]), jnp.float32),
        jnp.zeros((normed.shape[1],), jnp.bfloat16),
    )
    product, full_gain = add_piece(
        initial,
        (
            lax.all_gather(weight.astype(jnp.bfloat16), ("dp", "seq"), axis=0, tiled=True),
            lax.all_gather(gain.astype(jnp.bfloat16), ("dp", "seq"), axis=0, tiled=True),
        ),
        jnp.int32(0),
    )
    left = (normed * full_gain.astype(jnp.float32)).astype(jnp.bfloat16)
    return (product, left, None, full_gain.astype(jnp.float32))


def project_mid(left, weight):

    def add_piece(partial_sum, piece, start):
        return jnp.dot(left, piece, preferred_element_type=jnp.float32)

    initial = jnp.zeros((left.shape[0], weight.shape[1]), jnp.float32)
    product = add_piece(
        initial,
        lax.all_gather(weight.astype(jnp.bfloat16), ("dp", "seq"), axis=0, tiled=True),
        jnp.int32(0),
    )
    return (product, None)


def weights_back(upstream, weight):
    return contract_last(
        upstream, lax.all_gather(weight.astype(jnp.bfloat16), ("dp", "seq"), axis=0, tiled=True)
    )


def reduce_in(left, upstream):
    owned = left.shape[1] // lax.axis_size(("dp", "seq"))

    def term(start, count):
        return contract_rows(left, upstream)

    return lax.psum_scatter(
        term(jnp.int32(0), lax.axis_size(("dp", "seq")) * owned),
        ("dp", "seq"),
        scatter_dimension=0,
        tiled=True,
    )


def reduce_mid(left, upstream):
    owned = left.shape[1] // lax.axis_size(("dp", "seq"))

    def term(start, count):
        return contract_rows(left, upstream)

    return lax.psum_scatter(
        term(jnp.int32(0), lax.axis_size(("dp", "seq")) * owned),
        ("dp", "seq"),
        scatter_dimension=0,
        tiled=True,
    )


def gathered_body(
    tokens,
    cotangent,
    inner_weight,
    outer_weight,
    expand_weight,
    shrink_weight,
    norm_gains,
    first_inner,
    first_outer,
    first_expand,
    first_shrink,
    first_gains,
    second_inner,
    second_outer,
    second_expand,
    second_shrink,
    second_gains,
    document_index,
    group_order,
):
    inputs = tokens[0].astype(jnp.float32)
    rows, width = inputs.shape
    head_size = width // HEADS
    length = rows * lax.axis_size("seq")
    scale = head_size ** (-0.5)
    offset = -math.log(length)
    group = rows // 2
    within = jnp.arange(group, dtype=jnp.int32)
    paired = lax.dynamic_slice_in_dim(group_order, 2 * lax.axis_index("seq"), 2)
    own_place = (paired[:, None] * group + within[None, :]).reshape(-1)
    all_places = (group_order[:, None] * group + within[None, :]).reshape(-1)
    own_document = document_index[0].astype(jnp.bfloat16)
    cosine, sine = angles(own_place, head_size)
    inverse_first = lax.rsqrt(jnp.mean(inputs * inputs, axis=-1, keepdims=True) + EPSILON)
    normed_first = inputs * inverse_first
    projected, attend_input, kept_inner, gain_one = project_in(
        normed_first, inner_weight, norm_gains[0]
    )
    queries = projected[:, :width].reshape(rows, HEADS, head_size)
    query_rot = rotate(queries, cosine, sine).astype(jnp.bfloat16)
    key_rot = rotate(projected[:, width : 2 * width].reshape(rows, HEADS, head_size), cosine, sine)
    key_rot = key_rot.reshape(rows, width).astype(jnp.bfloat16)
    value_low = projected[:, 2 * width :].astype(jnp.bfloat16)

    def sigmoid_weights(key_piece, document_piece):
        count = key_piece.shape[0]
        scores = (
            jnp.einsum(
                "qhd,khd->hqk",
                query_rot,
                key_piece.reshape(count, HEADS, head_size),
                preferred_element_type=jnp.float32,
            )
            * scale
            + offset
        )
        visible = (own_document[:, None] == document_piece[None, :]) & (
            all_places[None, :] <= own_place[:, None]
        )
        return jax.nn.sigmoid(scores) * visible.astype(jnp.float32)[None]

    key_piece = lax.all_gather(key_rot, "seq", axis=0, tiled=True)
    value_piece = lax.all_gather(value_low, "seq", axis=0, tiled=True)
    document_piece = lax.all_gather(own_document, "seq", axis=0, tiled=True)
    count = key_piece.shape[0]
    weights = sigmoid_weights(key_piece, document_piece).astype(jnp.bfloat16)
    attended = jnp.einsum(
        "hqk,khd->qhd",
        weights,
        value_piece.reshape(count, HEADS, head_size),
        preferred_element_type=jnp.float32,
    )
    attended = attended.reshape(rows, width).astype(jnp.bfloat16)
    branch, kept_outer = project_mid(attended, outer_weight)
    residual = inputs + branch
    inverse_second = lax.rsqrt(jnp.mean(residual * residual, axis=-1, keepdims=True) + EPSILON)
    normed_second = residual * inverse_second
    gate_up, mlp_input, kept_expand, gain_two = project_in(
        normed_second, expand_weight, norm_gains[1]
    )
    hidden = gate_up.shape[1] // 2
    gate = gate_up[:, :hidden]
    upward = gate_up[:, hidden:]
    squash = jax.nn.sigmoid(gate)
    activation = (gate * squash * upward).astype(jnp.bfloat16)
    feed, kept_shrink = project_mid(activation, shrink_weight)
    output = residual + feed
    upstream = cotangent[0]
    down_grad = weights_back(upstream, shrink_weight)
    grad_shrink = reduce_mid(activation, upstream)
    d_gate = down_grad * upward * squash * (1.0 + gate * (1.0 - squash))
    d_upward = down_grad * gate * squash
    d_gate_up = jnp.concatenate([d_gate, d_upward], axis=1).astype(jnp.bfloat16)
    d_mlp_input = weights_back(d_gate_up, expand_weight)
    grad_expand = reduce_in(mlp_input, d_gate_up)
    partial_gain_two = jnp.sum(d_mlp_input * normed_second, axis=0)
    d_residual = upstream.astype(jnp.float32) + norm_back(
        d_mlp_input * gain_two, normed_second, inverse_second
    )
    d_residual_low = d_residual.astype(jnp.bfloat16)
    d_attended = weights_back(d_residual_low, outer_weight)
    grad_outer = reduce_mid(attended, d_residual_low)
    d_attended_flat = d_attended.astype(jnp.bfloat16)
    d_attended_low = d_attended_flat.reshape(rows, HEADS, head_size)
    key_piece = lax.all_gather(key_rot, "seq", axis=0, tiled=True)
    value_piece = lax.all_gather(value_low, "seq", axis=0, tiled=True)
    document_piece = lax.all_gather(own_document, "seq", axis=0, tiled=True)
    count = key_piece.shape[0]
    score_count = key_piece.shape[0]
    weights = sigmoid_weights(key_piece, document_piece)
    d_weights = jnp.einsum(
        "qhd,khd->hqk",
        d_attended_low,
        value_piece.reshape(score_count, HEADS, head_size),
        preferred_element_type=jnp.float32,
    )
    d_scores = (d_weights * weights * (1.0 - weights)).astype(jnp.bfloat16)
    weights, d_scores, key_heads = (
        weights,
        d_scores,
        key_piece.reshape(score_count, HEADS, head_size),
    )
    d_query = (
        jnp.einsum("hqk,khd->qhd", d_scores, key_heads, preferred_element_type=jnp.float32) * scale
    )
    key_term = (
        jnp.einsum("hqk,qhd->khd", d_scores, query_rot, preferred_element_type=jnp.float32) * scale
    )
    value_term = jnp.einsum(
        "hqk,qhd->khd",
        weights.astype(jnp.bfloat16),
        d_attended_low,
        preferred_element_type=jnp.float32,
    )
    d_keys = key_term.reshape(count, width)
    d_values = value_term.reshape(count, width)
    backward_sums = (d_query, d_keys, d_values)
    d_query = backward_sums[0]
    key_grad, value_grad = (
        lax.psum_scatter(
            backward_sums[1].astype(jnp.bfloat16), "seq", scatter_dimension=0, tiled=True
        ).astype(jnp.float32),
        lax.psum_scatter(
            backward_sums[2].astype(jnp.bfloat16), "seq", scatter_dimension=0, tiled=True
        ).astype(jnp.float32),
    )
    d_projected = jnp.concatenate(
        [
            unrotate(d_query, cosine, sine).reshape(rows, width),
            unrotate(key_grad.reshape(rows, HEADS, head_size), cosine, sine).reshape(rows, width),
            value_grad,
        ],
        axis=1,
    ).astype(jnp.bfloat16)
    d_attend_input = weights_back(d_projected, inner_weight)
    grad_inner = reduce_in(attend_input, d_projected)
    partial_gain_one = jnp.sum(d_attend_input * normed_first, axis=0)
    input_gradient = d_residual + norm_back(d_attend_input * gain_one, normed_first, inverse_first)
    local_squares = (
        jnp.sum(grad_inner * grad_inner)
        + jnp.sum(grad_outer * grad_outer)
        + jnp.sum(grad_expand * grad_expand)
    )
    local_squares = local_squares + jnp.sum(grad_shrink * grad_shrink)
    matrix_squares, gains_whole = lax.psum(
        (local_squares, jnp.stack([partial_gain_one, partial_gain_two])), ("dp", "seq")
    )
    owned_gains = norm_gains.shape[1]
    grad_gains = lax.dynamic_slice_in_dim(
        gains_whole, lax.axis_index(("dp", "seq")) * owned_gains, owned_gains, 1
    )
    global_norm = jnp.sqrt(matrix_squares + jnp.sum(gains_whole * gains_whole))
    factor = CLIP / jnp.maximum(global_norm, CLIP)
    gradients = (grad_inner, grad_outer, grad_expand, grad_shrink, grad_gains)
    masters = (inner_weight, outer_weight, expand_weight, shrink_weight, norm_gains)
    firsts = (first_inner, first_outer, first_expand, first_shrink, first_gains)
    seconds = (second_inner, second_outer, second_expand, second_shrink, second_gains)
    decays = (DECAY, DECAY, DECAY, DECAY, 0.0)
    rates = (RATE, RATE, RATE, RATE, GAIN_RATE)
    results = [
        adamw(
            masters[index],
            gradients[index],
            firsts[index],
            seconds[index],
            factor,
            decays[index],
            rates[index],
        )
        for index in range(5)
    ]
    return (
        output[None],
        input_gradient[None],
        global_norm,
        results[0][0],
        results[1][0],
        results[2][0],
        results[3][0],
        results[4][0],
        results[0][1],
        results[1][1],
        results[2][1],
        results[3][1],
        results[4][1],
        results[0][2],
        results[1][2],
        results[2][2],
        results[3][2],
        results[4][2],
    )


def solution(mesh):
    whole_heads = mesh.shape["seq"] == 2 * DEPTH and mesh.shape["dp"] == 4
    placed = (
        P("dp", "seq", None),
        P("dp", "seq", None),
        P(("dp", "seq"), None),
        P(("dp", "seq"), None),
        P(("dp", "seq"), None),
        P(("dp", "seq"), None),
        P(None, ("dp", "seq")),
        P(("dp", "seq"), None),
        P(("dp", "seq"), None),
        P(("dp", "seq"), None),
        P(("dp", "seq"), None),
        P(None, ("dp", "seq")),
        P(("dp", "seq"), None),
        P(("dp", "seq"), None),
        P(("dp", "seq"), None),
        P(("dp", "seq"), None),
        P(None, ("dp", "seq")),
        P("dp", "seq"),
        P(),
    )
    return jax.shard_map(
        body if whole_heads else gathered_body,
        mesh=mesh,
        in_specs=placed,
        out_specs=(
            P("dp", "seq", None),
            P("dp", "seq", None),
            P(),
            P(("dp", "seq"), None),
            P(("dp", "seq"), None),
            P(("dp", "seq"), None),
            P(("dp", "seq"), None),
            P(None, ("dp", "seq")),
            P(("dp", "seq"), None),
            P(("dp", "seq"), None),
            P(("dp", "seq"), None),
            P(("dp", "seq"), None),
            P(None, ("dp", "seq")),
            P(("dp", "seq"), None),
            P(("dp", "seq"), None),
            P(("dp", "seq"), None),
            P(("dp", "seq"), None),
            P(None, ("dp", "seq")),
        ),
        check_vma=False,
    )
```
